32 devices in a mesh: pipe: 4 (over y, core), dp: 8 (over z, x).
Axes of the slice: x: 2, y: 2, z: 4, core: 2. Of those that a mesh axis runs over, the one named last changes fastest.
Arguments:
- tokens_in: bfloat16 [35840, 256], P('dp'), may hold values from -6 to 6
- cotangent: bfloat16 [35840, 256], P('dp'), may hold values from -6 to 6
- valid_mask: int32 [128, 280], P('dp'), may hold values from 0 to 1, as said below
- orientation: int32 [128], P('dp'), may hold values from 0 to 1
- dilation: int32 [128, 2], P('dp'), may hold values from 1 to 2
- norm_gain: bfloat16 [4, 256], P('pipe'), may hold values from 0.25 to 1.75
- norm_bias: bfloat16 [4, 256], P('pipe'), may hold values from -1.5 to 1.5
- in_weight: bfloat16 [4, 256, 768], P('pipe'), may hold values from -0.375 to 0.375
- in_bias: bfloat16 [4, 768], P('pipe'), may hold values from -1.5 to 1.5
- out_bias: bfloat16 [4, 256], P('pipe'), may hold values from -1.5 to 1.5
- proj_weight: bfloat16 [2, 256, 256], replicated, may hold values from -1.5 to 1.5
- down_weight: bfloat16 [2, 768, 256], replicated, may hold values from -0.21875 to 0.21875
- position_bias: bfloat16 [2, 8, 169], replicated, may hold values from -4 to 4
Outputs:
- section_outputs: bfloat16 [4, 35840, 256], P('pipe', 'dp')
- section_input_grads: bfloat16 [4, 35840, 256], P('pipe', 'dp')
- grad_norm_gain: float32 [4, 256], P('pipe')
- grad_norm_bias: float32 [4, 256], P('pipe')
- grad_in_weight: float32 [4, 256, 768], P('pipe')
- grad_in_bias: float32 [4, 768], P('pipe')
- grad_out_bias: float32 [4, 256], P('pipe')
- grad_proj: float32 [2, 256, 256], replicated
- grad_down: float32 [2, 768, 256], replicated
- grad_position_bias: float32 [2, 8, 169], replicated
The draws below stay inside these ranges and needn't reach their ends.
Inputs may be any that keep to these rules, and one draw needn't show every extreme that they name: `valid_mask`: each image's valid tokens are the grid rows 0 to r - 1 and columns 0 to c - 1, with 8 <= r <= 14 and 14 <= c <= 20.
All inputs are finite; a program needn't handle non-finite values.
Results may differ from the reference program's by a relative error of at most 0.017.
Values may be sent and summed in bfloat16 or wider, within the bound.
A program may use at most 448 MiB of HBM per device.

```python
import jax
import jax.numpy as jnp
from jax import lax

D = 256
HEADS = 8
HEAD = 32
FF = 768
KS = 7
R_SIDE = 14
C_SIDE = 20
BLOCKS = 2
PIX = 280
RB = 169
IMAGES = 128
TOKENS = 35840


def draw_valid_mask(key, part):
    key = jax.random.fold_in(key, 11)
    key_rows, key_cols = jax.random.split(key)
    rows_valid = jax.random.randint(key_rows, (IMAGES, 1), R_SIDE - 6, R_SIDE + 1)
    cols_valid = jax.random.randint(key_cols, (IMAGES, 1), C_SIDE - 6, C_SIDE + 1)
    places = jnp.arange(PIX, dtype=jnp.int32)
    row_of = places // C_SIDE
    col_of = places % C_SIDE
    inside = (row_of[None, :] < rows_valid) & (col_of[None, :] < cols_valid)
    return inside.astype(jnp.int32)


def set_ends(values, rng, least, high):
    dims = values.shape
    index_at = [jax.random.randint(jax.random.fold_in(rng, axis), (), 0, dims[axis]) for axis in range(len(dims))]
    values = values.at[tuple(index_at)].set(least)
    longest = dims.index(max(dims))
    index_at[longest] = (index_at[longest] + 1) % dims[longest]
    return values.at[tuple(index_at)].set(high)


def level_of(stream_key, shape, pieces, low, high):
    loudness = 1.0
    for axis_at, parts in pieces:
        heights = jax.random.uniform(jax.random.fold_in(jax.random.fold_in(stream_key, 6), axis_at), (parts,), jnp.float32, low / len(pieces), high / len(pieces))
        loudness = loudness * jnp.repeat(jnp.exp(heights), shape[axis_at] // parts).reshape((-1,) + (1,) * (len(shape) - 1 - axis_at))
    return loudness


def scatter_about(key, shape, deviation, bound, cuts=(), kind=jnp.bfloat16):
    values = jax.random.normal(key, shape, jnp.float32) * deviation
    if len(cuts) > 0:
        values = level_of(key, shape, cuts, -0.22, 0.18) * values
    return jnp.clip(values, min=-bound, max=bound).astype(kind)


def setup_inputs(seed: int = 0) -> dict:
    seeds = jax.random.split(jax.random.key(seed), 14)
    return {
        "tokens_in": scatter_about(seeds[0], (TOKENS, D), 1.0, 6.0, ((0, 8),)),
        "cotangent": scatter_about(seeds[1], (TOKENS, D), 1.0, 6.0, ((0, 8),)),
        "valid_mask": draw_valid_mask(jax.random.fold_in(seeds[13], 71), 0),
        "orientation": set_ends(jax.random.randint(seeds[3], (IMAGES,), 0, 2), jax.random.fold_in(seeds[3], 1), 0, 1).astype(jnp.int32),
        "dilation": set_ends(jax.random.randint(seeds[4], (IMAGES, BLOCKS), 1, 3), jax.random.fold_in(seeds[4], 1), 1, 2).astype(jnp.int32),
        "norm_gain": jnp.clip(1.0 + 0.15 * jax.random.normal(seeds[5], (2 * BLOCKS, D), jnp.float32), 0.25, 1.75).astype(jnp.bfloat16),
        "norm_bias": scatter_about(seeds[6], (2 * BLOCKS, D), 0.3, 1.5, ((0, 4),)),
        "in_weight": scatter_about(seeds[7], (2 * BLOCKS, D, FF), D ** -0.5, 0.375, ((0, 4),)),
        "in_bias": scatter_about(seeds[8], (2 * BLOCKS, FF), 0.3, 1.5, ((0, 4),)),
        "out_bias": scatter_about(seeds[9], (2 * BLOCKS, D), 0.3, 1.5, ((0, 4),)),
        "proj_weight": scatter_about(seeds[10], (BLOCKS, D, D), (D // 16) ** -0.5, 1.5),
        "down_weight": scatter_about(seeds[11], (BLOCKS, FF, D), FF ** -0.5, 0.21875),
        "position_bias": scatter_about(seeds[12], (BLOCKS, HEADS, RB), 1.0, 4.0),
    }


@jax.custom_vjp
def low(v):
    return lax.optimization_barrier(v.astype(jnp.bfloat16)).astype(jnp.float32)

@jax.custom_vjp
def low_back(v):
    return v

def low_keep(v):
    return (low(v), None)

def low_pass(kept, grad):
    return (grad,)

def back_keep(v):
    return (v, None)

def back_low(kept, grad):
    return (low(grad),)
low.defvjp(low_keep, low_pass)
low_back.defvjp(back_keep, back_low)
EPS = 1e-05
NEG = -1e+30
HIGH = lax.Precision.HIGHEST

def norm_rows(x, gain, shift):
    center = x - lax.optimization_barrier(jnp.mean(x, axis=-1, keepdims=True))
    spread = lax.optimization_barrier(jnp.mean(center * center, axis=-1, keepdims=True))
    return center * lax.rsqrt(spread + EPS) * gain + shift

def window_tables(spacing_in, length):
    places = jnp.arange(length, dtype=jnp.int32)
    spacing = spacing_in.astype(jnp.int32)[:, None]
    group = places[None, :] % spacing
    local = places[None, :] // spacing
    count = (length - group + spacing - 1) // spacing
    start = jnp.clip(local - KS // 2, 0, count - KS)
    same = group[:, :, None] == group[:, None, :]
    reach = local[:, None, :] - start[:, :, None]
    inside = same & (reach >= 0) & (reach < KS)
    offset = local[:, None, :] - local[:, :, None] + KS - 1
    ladder = jnp.arange(2 * KS - 1, dtype=jnp.int32)
    onehot = (inside[..., None] & (offset[..., None] == ladder)).astype(jnp.float32)
    return (inside, onehot)

def geometry(mask, turn, spacing):
    count = mask.shape[0]
    row_in, row_hot = window_tables(spacing, R_SIDE)
    col_in, col_hot = window_tables(spacing, C_SIDE)
    valid = mask.reshape(count, R_SIDE, C_SIDE) > 0
    allowed = row_in[:, :, None, :, None] & col_in[:, None, :, None, :] & valid[:, None, None, :, :]
    return (allowed.reshape(count, PIX, PIX), row_hot, col_hot, turn)

def head_bias(table, geo):
    allowed, row_hot, col_hot, turn = geo
    turned = jnp.where(turn[:, None, None] == 1, table.T[None], table[None])
    first = jnp.einsum('nxua,nab->nxub', row_hot, turned, precision=HIGH)
    full = jnp.einsum('nxub,nyvb->nxyuv', first, col_hot, precision=HIGH)
    return full.reshape(allowed.shape)

def attend_head(query, keys, values, table, geo):
    raw = low_back(jnp.einsum('npe,nke->npk', query, keys, precision=HIGH))
    scores = jnp.where(geo[0], raw + head_bias(table, geo), NEG)
    top = lax.optimization_barrier(jnp.max(scores, axis=-1, keepdims=True))
    expo = jnp.exp(scores - top)
    prob = expo / lax.optimization_barrier(jnp.sum(expo, axis=-1, keepdims=True))
    return jnp.einsum('npk,nke->npe', low(prob), values, precision=HIGH)

def split_heads(matrix, count):
    return matrix.reshape(count, PIX, HEADS, HEAD).transpose(2, 0, 1, 3)

def attention_section(x, gain, shift, w_in, b_in, w_proj, b_out, tables, geo):
    width = x.shape[1]
    count = geo[0].shape[0]
    normed = low(norm_rows(x, gain, shift))
    mixed = low_back(jnp.dot(normed, w_in, precision=HIGH) + b_in)
    query = low(mixed[:, :width] * HEAD ** (-0.5))
    keys = low(mixed[:, width:2 * width])
    values = low(mixed[:, 2 * width:])

    def one_head(item):
        return attend_head(item[0], item[1], item[2], item[3], geo)
    heads = lax.map(jax.checkpoint(one_head), (split_heads(query, count), split_heads(keys, count), split_heads(values, count), tables))
    attended = heads.transpose(1, 2, 0, 3).reshape(x.shape[0], width)
    attended = low(low_back(attended))
    return x + jnp.dot(attended, w_proj, precision=HIGH) + b_out

def mlp_section(x, gain, shift, w_in, b_in, w_down, b_out):
    normed = low(norm_rows(x, gain, shift))
    hidden = low_back(jnp.dot(normed, w_in, precision=HIGH) + b_in)
    active = low(jax.nn.gelu(hidden, approximate=False))
    return x + jnp.dot(active, w_down, precision=HIGH) + b_out

def forward(params, extras, xin, mask, turn, spacing):
    gains, shifts, w_ins, b_ins, b_outs, w_projs, w_downs, biases = params
    span = 2 * KS - 1
    geos = [geometry(mask, turn, spacing[:, block]) for block in range(BLOCKS)]
    outputs = []
    current = xin
    for section in range(2 * BLOCKS):
        block = section // 2
        inner = low_back(current + extras[section])
        if section % 2 == 0:
            result = attention_section(inner, gains[section], shifts[section], w_ins[section], b_ins[section], w_projs[block], b_outs[section], biases[block].reshape(HEADS, span, span), geos[block])
        else:
            result = mlp_section(inner, gains[section], shifts[section], w_ins[section], b_ins[section], w_downs[block], b_outs[section])
        outputs.append(result)
        current = low(result)
    return tuple(outputs)

def reference(tokens_in, cotangent, valid_mask, orientation, dilation, norm_gain, norm_bias, in_weight, in_bias, out_bias, proj_weight, down_weight, position_bias):
    group_images = 8
    groups = IMAGES // group_images
    rows = group_images * PIX
    width = tokens_in.shape[1]
    params = tuple((p.astype(jnp.float32) for p in (norm_gain, norm_bias, in_weight, in_bias, out_bias, proj_weight, down_weight, position_bias)))
    inputs = tokens_in.astype(jnp.float32).reshape(groups, rows, width)
    grads_in = cotangent.astype(jnp.float32).reshape(groups, rows, width)
    masks = valid_mask.reshape(groups, group_images, PIX)
    turns = orientation.reshape(groups, group_images)
    spacings = dilation.reshape(groups, group_images, BLOCKS)

    def group_step(totals, item):
        xin, upstream, mask, turn, spacing = item
        empty = jnp.zeros((rows, width), jnp.float32)

        def run(values, e_zero, e_one, e_two, e_three):
            return forward(values, (e_zero, e_one, e_two, e_three), xin, mask, turn, spacing)
        results, pullback = jax.vjp(run, params, empty, empty, empty, empty)
        grads = pullback((empty, empty, empty, upstream))
        totals = jax.tree.map(lambda a, b: a + b, totals, grads[0])
        outs = jnp.stack([r.astype(jnp.bfloat16) for r in results])
        backs = jnp.stack([g.astype(jnp.bfloat16) for g in grads[1:]])
        return (totals, (outs, backs))
    start = jax.tree.map(jnp.zeros_like, params)
    totals, (outs, backs) = lax.scan(group_step, start, (inputs, grads_in, masks, turns, spacings))
    section_outputs = outs.transpose(1, 0, 2, 3).reshape(2 * BLOCKS, TOKENS, width)
    section_input_grads = backs.transpose(1, 0, 2, 3).reshape(2 * BLOCKS, TOKENS, width)
    return (section_outputs, section_input_grads, totals[0], totals[1], totals[2], totals[3], totals[4], totals[5], totals[6], totals[7])
```

```python
import functools
import math

import jax
import jax.numpy as jnp
import ml_dtypes
import numpy as np
from jax import lax
from jax.experimental import pallas as pl
from jax.experimental.pallas import tpu as pltpu
from jax.sharding import PartitionSpec as P

HEADS = 8
HEAD = 32
KS = 7
R_SIDE = 14
C_SIDE = 20
PIX = 280
SPAN = 13
EPS = 1e-05
NEG = -1e30
HALF = 144
PAD = 288
OWN = 140
LAG = 1
LATE_PAIR = 3
QUERY_AT = (0, 136)
KEY_AT = (0, 32)
LOG2E = math.log2(math.e)
LN2 = math.log(2.0)
F32 = jnp.float32
BF16 = jnp.bfloat16


def token_places(dilation):
    place = np.arange(PIX)
    if dilation == 1:
        return place // C_SIDE, place % C_SIDE
    row_class, rest = place // OWN, place % OWN
    row_local, rest = rest // C_SIDE, rest % C_SIDE
    col_class, col_local = rest // 10, rest % 10
    return row_local * 2 + row_class, col_local * 2 + col_class


def line_window(q, k, dilation, length):
    same = (q % dilation) == (k % dilation)
    count = (length - q % dilation + dilation - 1) // dilation
    start = np.clip(q // dilation - KS // 2, 0, count - KS)
    reach = k // dilation - start
    return same & (reach >= 0) & (reach < KS)


def constant_tables():
    window = np.zeros((2, 2, HALF, 256), np.float32)
    lane_row = np.full((2, 2, 8, 256), 1000, np.int32)
    lane_col = np.full((2, 2, 8, 256), 1000, np.int32)
    perm = np.zeros((2, PAD, PAD), np.float32)
    for d in (1, 2):
        rows, cols = token_places(d)
        perm[d - 1, np.arange(PIX), rows * C_SIDE + cols] = 1
        for half in (0, 1):
            keys = KEY_AT[half] + np.arange(256)
            real = keys < PIX
            key_row = np.where(real, rows[np.minimum(keys, PIX - 1)], 1000)
            key_col = np.where(real, cols[np.minimum(keys, PIX - 1)], 1000)
            query = half * OWN + np.arange(OWN)
            inside = (
                line_window(rows[query][:, None], key_row[None], d, R_SIDE)
                & line_window(cols[query][:, None], key_col[None], d, C_SIDE)
                & real[None]
            )
            window[d - 1, half, query - QUERY_AT[half]] = np.where(inside, 0.0, NEG)
            lane_row[d - 1, half] = key_row[None]
            lane_col[d - 1, half] = key_col[None]
    pick = np.zeros((2, 256, 512), np.float32)
    for m in range(-6, 7):
        for w in range(-6, 7):
            gap = 20 * m + w
            for turn in (0, 1):
                entry = (m + 6) * SPAN + w + 6 if turn == 0 else (w + 6) * SPAN + m + 6
                for half in (0, 1):
                    pick[turn, entry, half * 256 + (gap + QUERY_AT[half] - KEY_AT[half]) % 256] = 1
    low = ml_dtypes.bfloat16
    return (
        window.astype(low),
        lane_row,
        lane_col,
        perm.astype(low),
        perm.transpose(0, 2, 1).astype(low),
        pick.astype(low),
    )


def dot_nn(a, b):
    return lax.dot_general(a, b, (((1,), (0,)), ((), ())), preferred_element_type=F32)


def dot_nt(a, b):
    return lax.dot_general(a, b, (((1,), (1,)), ((), ())), preferred_element_type=F32)


def dot_tn(a, b):
    return lax.dot_general(a, b, (((0,), (0,)), ((), ())), preferred_element_type=F32)


def lane_ids(shape):
    return lax.broadcasted_iota(jnp.int32, shape, len(shape) - 1)


def normalise(x):
    center = x - jnp.mean(x, axis=-1, keepdims=True)
    rstd = lax.rsqrt(jnp.mean(center * center, axis=-1, keepdims=True) + EPS)
    return center * rstd, rstd


def gelu_pair(h):
    phi = 0.5 + 0.5 * lax.erf(h * math.sqrt(0.5))
    e = jnp.exp2(h * h * (-0.5 * LOG2E))
    return h * phi, phi + h * (e * (1.0 / math.sqrt(2.0 * math.pi)))


def mask_heads(rows):
    lanes = lane_ids((1, 256)) // HEAD
    return jnp.concatenate([rows * jnp.where(lanes == h, 1.0, 0.0).astype(BF16) for h in range(HEADS)], axis=0)


def pick_heads(stack):
    lanes = lane_ids((HALF, 128)) // HEAD
    total = stack[0:HALF]
    for h in range(1, 4):
        total = jnp.where(lanes == h, stack[h * HALF : (h + 1) * HALF], total)
    return total


def diagonal_sums(left, right):
    lanes = lane_ids((8, 128))
    low = jnp.zeros((8, 128), F32)
    high = jnp.zeros((8, 128), F32)
    for t in range(HALF // 8):
        shift = (8 * t) % 128
        a = left[8 * t : 8 * t + 8]
        b = right[8 * t : 8 * t + 8]
        if 8 * t >= 128:
            a, b = b, a
        if shift:
            a = pltpu.roll(a, 128 - shift, 1)
            b = pltpu.roll(b, 128 - shift, 1)
            near = lanes < 128 - shift
            a, b = jnp.where(near, a, b), jnp.where(near, b, a)
        low = low + a
        high = high + b
    return low, high


def together(*works):
    works = list(works)
    while works:
        for work in list(works):
            if next(work, None) is None:
                works.remove(work)


def join_halves(first, second):
    upper = lax.broadcasted_iota(jnp.int32, (8, first.shape[1]), 0) < 4
    seam = jnp.where(upper, first[136:144], second[0:8])
    tail = jnp.zeros((8, first.shape[1]), first.dtype)
    return jnp.concatenate([first[0:136], seam, second[8:144], tail], axis=0)


def own_rows(rows, half):
    upper = lax.broadcasted_iota(jnp.int32, (8, rows.shape[1]), 0) < 4
    if half == 0:
        return jnp.concatenate([rows[0:136], jnp.where(upper, rows[136:144], 0.0)], axis=0)
    return jnp.concatenate([jnp.where(upper, 0.0, rows[0:8]), rows[8:144]], axis=0)


def mesh_copy(src, dst, send, recv, pipe, dp):
    return pltpu.make_async_remote_copy(
        src_ref=src,
        dst_ref=dst,
        send_sem=send,
        recv_sem=recv,
        device_id=(pipe, dp),
        device_id_type=pl.DeviceIdType.MESH,
    )


def await_bytes(like, sem):
    pltpu.make_async_copy(like, like, sem).wait()


class Pack:
    def __init__(self, dp, refs, sems):
        self.pairs = dp // 2
        self.acc, self.send, self.core, self.side, self.cut, self.gather, self.total = refs
        self.core_send, self.core_recv, self.side_send, self.side_recv, self.cut_send, self.cut_recv = sems[0:6]
        self.all_send = sems[6:8]
        self.p = lax.axis_index("pipe")
        self.me = lax.axis_index("dp")
        self.c = lax.rem(self.p, 2)
        self.x = lax.rem(self.me, 2)
        self.z = lax.div(self.me, 2)
        self.sibling = self.p + 1 - 2 * self.c
        self.across = lax.rem(self.p + 2, 4)
        self.partner = self.me + 1 - 2 * self.x

    def owner(self, work):
        if self.pairs == 4:
            work()
        else:
            pl.when(self.z < 4)(work)

    def half(self, core):
        return pl.ds(pl.multiple_of(128 * core, 128), 128)

    def quarter(self, side):
        return pl.ds(pl.multiple_of(128 * self.c + 64 * side, 64), 64)

    def core_copy(self, k):
        return mesh_copy(
            self.send.at[k, self.half(1 - self.c)],
            self.core.at[k],
            self.core_send.at[k],
            self.core_recv.at[k],
            self.sibling,
            self.me,
        )

    def side_copy(self, k):
        return mesh_copy(
            self.send.at[k, self.quarter(1 - self.x)],
            self.side.at[k],
            self.side_send.at[k],
            self.side_recv.at[k],
            self.p,
            self.partner,
        )

    def start_core(self, k):
        self.send[k] = self.acc[k].astype(BF16)
        self.core_copy(k).start()

    def start_side(self, k):
        self.core_copy(k).wait_recv()
        rows = self.half(self.c)
        self.send[k, rows] = (self.send[k, rows].astype(F32) + self.core[k].astype(F32)).astype(BF16)
        self.side_copy(k).start()

    def start_cut(self, k):
        self.side_copy(k).wait_recv()
        summed = self.send[k, self.quarter(self.x)].astype(F32) + self.side[k].astype(F32)
        self.cut[k] = summed.astype(BF16).reshape(self.cut.shape[1:])

        @self.owner
        def _():
            self.gather[k, self.z] = self.cut[k, self.z]

        def send_piece(j, carry):
            @pl.when(j != self.z)
            def _():
                mesh_copy(
                    self.cut.at[k, j],
                    self.gather.at[k, self.z],
                    self.cut_send.at[k],
                    self.cut_recv.at[k],
                    self.p,
                    2 * j + self.x,
                ).start()

            return carry

        lax.fori_loop(0, 4, send_piece, 0)

    def sum_pieces(self, k):
        @self.owner
        def _():
            await_bytes(self.gather.at[k, pl.ds(0, self.pairs - 1)], self.cut_recv.at[k])

            def add(j, total):
                return total + self.gather[k, j].astype(F32)

            zero = jnp.zeros(self.total.shape[1:], F32)
            self.total[k] = lax.fori_loop(0, self.pairs, add, zero).astype(BF16)

    def start_gather(self, k, place, recv, pipe, far=None):
        def send_piece(j, carry):
            local = (pipe == self.p) & (j == self.z)

            @pl.when(local)
            def _():
                pltpu.make_async_copy(self.total.at[k], place, recv).start()

            @pl.when(jnp.logical_not(local))
            def _():
                mesh_copy(self.total.at[k], place, self.all_send[0].at[k], recv, pipe, 2 * j + self.x).start()

            if far is not None:

                @pl.when(far)
                def _():
                    mesh_copy(
                        self.total.at[k], place, self.all_send[1].at[k], recv, self.across, 2 * j + self.x
                    ).start()

            return carry

        @self.owner
        def _():
            lax.fori_loop(0, self.pairs, send_piece, 0)

    def finish_sends(self, k, pipe, far=None):
        self.core_copy(k).wait_send()
        self.side_copy(k).wait_send()

        @self.owner
        def _():
            await_bytes(self.cut.at[k, pl.ds(0, 3)], self.cut_send.at[k])

            @pl.when(pipe == self.p)
            def _():
                await_bytes(self.gather.at[k, pl.ds(0, self.pairs - 1)], self.all_send[0].at[k])

            @pl.when(pipe != self.p)
            def _():
                await_bytes(self.gather.at[k], self.all_send[0].at[k])

            if far is not None:

                @pl.when(far)
                def _():
                    await_bytes(self.gather.at[k], self.all_send[1].at[k])

        if self.pairs > 4:

            @pl.when(self.z >= 4)
            def _():
                await_bytes(self.cut.at[k], self.cut_send.at[k])


class Direct:
    def __init__(self, dp, refs, sems):
        self.dp = dp
        self.acc, self.send, self.core, self.cut, self.gather, self.total = refs
        self.core_send, self.core_recv, self.cut_send, self.cut_recv, self.all_send = sems
        self.p = lax.axis_index("pipe")
        self.me = lax.axis_index("dp")
        self.c = lax.rem(self.p, 2)
        self.sibling = self.p + 1 - 2 * self.c
        self.goal = self.p - self.c

    def owner(self, work):
        if self.dp == 8:
            work()
        else:
            pl.when(self.me < 8)(work)

    def half(self, core):
        return pl.ds(pl.multiple_of(128 * core, 128), 128)

    def core_copy(self):
        source = self.send.at[self.half(1 - self.c)]
        return mesh_copy(source, self.core, self.core_send, self.core_recv, self.sibling, self.me)

    def start_core(self):
        self.send[...] = self.acc[...].astype(BF16)
        self.core_copy().start()

    def start_cut(self):
        self.core_copy().wait_recv()
        summed = self.send[self.half(self.c)].astype(F32) + self.core[...].astype(F32)
        self.cut[...] = summed.astype(BF16).reshape(self.cut.shape)

        @self.owner
        def _():
            self.gather[self.me] = self.cut[self.me]

        def send_piece(j, carry):
            @pl.when(j != self.me)
            def _():
                place = self.gather.at[self.me]
                mesh_copy(self.cut.at[j], place, self.cut_send, self.cut_recv, self.p, j).start()

            return carry

        lax.fori_loop(0, 8, send_piece, 0)

    def start_gather(self, land, recv):
        place = land.at[pl.ds(pl.multiple_of(128 * self.c + 16 * self.me, 16), 16)]

        def send_piece(j, carry):
            local = (self.c == 0) & (j == self.me)

            @pl.when(local)
            def _():
                pltpu.make_async_copy(self.total, place, recv).start()

            @pl.when(jnp.logical_not(local))
            def _():
                mesh_copy(self.total, place, self.all_send, recv, self.goal, j).start()

            return carry

        @self.owner
        def _():
            await_bytes(self.gather.at[pl.ds(0, self.dp - 1)], self.cut_recv)

            def add(j, total):
                return total + self.gather[j].astype(F32)

            self.total[...] = lax.fori_loop(0, self.dp, add, jnp.zeros(self.total.shape, F32)).astype(BF16)
            lax.fori_loop(0, self.dp, send_piece, 0)

    def finish_sends(self):
        self.core_copy().wait_send()

        @self.owner
        def _():
            await_bytes(self.cut.at[pl.ds(0, 7)], self.cut_send)

            @pl.when(self.c == 0)
            def _():
                await_bytes(self.gather.at[pl.ds(0, self.dp - 1)], self.all_send)

            @pl.when(self.c == 1)
            def _():
                await_bytes(self.gather, self.all_send)

        if self.dp > 8:

            @pl.when(self.me >= 8)
            def _():
                await_bytes(self.cut, self.cut_send)


def section_kernel(
    images,
    dp,
    mask_ref,
    turn_ref,
    dil_ref,
    tok_hbm,
    cot_hbm,
    win_hbm,
    gain_ref,
    shift_ref,
    bin_ref,
    bout_ref,
    table_ref,
    proj_hbm,
    down_hbm,
    window_hbm,
    lrow_hbm,
    lcol_hbm,
    perm_hbm,
    permt_hbm,
    pick_hbm,
    out_hbm,
    back_hbm,
    sum_in_hbm,
    sum_down_hbm,
    notes_hbm,
    land_in,
    land_down,
    notes_ref,
    proj_ref,
    down_ref,
    window_ref,
    lrow_ref,
    lcol_ref,
    perm_ref,
    permt_ref,
    pick_ref,
    nat_ref,
    xhat_ref,
    rstd_ref,
    qkv_ref,
    prob_ref,
    att_ref,
    act_ref,
    slope_ref,
    up_ref,
    inverse_ref,
    ones_ref,
    maskadd_ref,
    bias_ref,
    tab_ref,
    diag_ref,
    win_ref,
    small_ref,
    gs_ref,
    give_ref,
    load_ref,
    wide_acc,
    wide_send,
    wide_core,
    wide_side,
    wide_cut,
    wide_gather,
    wide_total,
    slim_acc,
    slim_send,
    slim_core,
    slim_side,
    slim_cut,
    slim_gather,
    slim_total,
    tall_send,
    tall_core,
    tall_cut,
    tall_gather,
    tall_total,
    note_send,
    note_core,
    note_side,
    note_all,
    note_far,
    load_sem,
    const_sems,
    win_sems,
    small_sems,
    give_send,
    give_recv,
    cross_send,
    cross_recv,
    wide_sems,
    slim_sems,
    tall_sems,
    land_sems,
    share_send,
    share_recv,
    side_send,
    side_recv,
    far_send,
    far_recv,
    note_sems,
):
    p = lax.axis_index("pipe")
    me = lax.axis_index("dp")
    core = lax.rem(p, 2)
    block = lax.div(p, 2)
    sibling = p + 1 - 2 * core
    across = lax.rem(p + 2, 4)
    first = core * images
    rows_own = images * PIX
    pair_rows = 2 * PIX
    wide = Pack(
        dp,
        (wide_acc.at[pl.ds(1, 1)], wide_send, wide_core, wide_side, wide_cut, wide_gather, wide_total),
        [wide_sems.at[n] for n in range(8)],
    )
    slim = Pack(
        dp,
        (slim_acc, slim_send, slim_core, slim_side, slim_cut, slim_gather, slim_total),
        [slim_sems.at[n] for n in range(8)],
    )
    tall = Direct(
        dp,
        (wide_acc.at[0], tall_send, tall_core, tall_cut, tall_gather, tall_total),
        [tall_sems.at[n] for n in range(5)],
    )

    constants = (
        (window_hbm, window_ref),
        (lrow_hbm, lrow_ref),
        (lcol_hbm, lcol_ref),
        (perm_hbm, perm_ref),
        (permt_hbm, permt_ref),
        (proj_hbm.at[block], proj_ref),
        (down_hbm.at[block], down_ref),
    )
    constants = [
        pltpu.make_async_copy(source, target, const_sems.at[n]) for n, (source, target) in enumerate(constants)
    ]
    pick_load = pltpu.make_async_copy(pick_hbm, pick_ref, const_sems.at[len(constants)])

    barrier = pltpu.get_barrier_semaphore()
    side = lax.rem(me, 2)
    pair_of = lax.div(me, 2)
    partner = me + 1 - 2 * side

    def greet_one(pipe, dp_index):
        pl.semaphore_signal(
            barrier, inc=1, device_id=(pipe, dp_index), device_id_type=pl.DeviceIdType.MESH
        )

    def greet(j, carry):
        greet_one(sibling, j)
        pl.when(j != me)(lambda: greet_one(p, j))
        pl.when(lax.rem(j, 2) == side)(lambda: greet_one(across, j))
        return carry

    lax.fori_loop(0, dp, greet, 0)

    mine = pl.ds(pl.multiple_of(core * rows_own, 16), rows_own)
    win_load = pltpu.make_async_copy(win_hbm.at[0], win_ref.at[core], load_sem.at[0])
    win_load.start()
    pick_load.start()
    tok_load = pltpu.make_async_copy(tok_hbm.at[mine], load_ref, load_sem.at[1])
    cot_load = pltpu.make_async_copy(cot_hbm.at[mine], load_ref, load_sem.at[1])
    pl.when(block == 0)(tok_load.start)
    pl.when(block == 1)(cot_load.start)
    for copy in constants:
        copy.start()
    small_ref[core, 0:1] = gain_ref[...].astype(F32)
    small_ref[core, 1:2] = shift_ref[...].astype(F32)
    small_ref[core, 2:3] = bout_ref[...].astype(F32)
    for part in range(3):
        small_ref[core, 3 + part : 4 + part] = bin_ref[:, part * 256 : part * 256 + 256].astype(F32)
    pl.semaphore_wait(barrier, 2 * dp - 1 + dp // 2)
    win_copy = mesh_copy(win_ref.at[core], win_ref.at[core], win_sems.at[0], win_sems.at[1], sibling, me)
    small_copy = mesh_copy(
        small_ref.at[core], small_ref.at[core], small_sems.at[0], small_sems.at[1], sibling, me
    )
    small_copy.start()
    win_load.wait()
    win_copy.start()

    tab_ref[...] = jnp.zeros_like(tab_ref)
    tab_ref[:, 0 : SPAN * SPAN] = table_ref[block].astype(F32)
    tab = tab_ref[...].astype(BF16)
    pick_load.wait()
    for turn in range(2):
        base = dot_nn(tab, pick_ref[turn]) * LOG2E
        for s in range(8):
            rows = pl.ds(turn * 8, 8)
            for half in range(2):
                ring = base[:, half * 256 : half * 256 + 256]
                ring = pltpu.roll(ring, s, 1) if s else ring
                diag_ref[2 * half, rows, s] = ring[:, 0:128]
                diag_ref[2 * half + 1, rows, s] = ring[:, 128:256]

    def spread(n, carry):
        lanes = lane_ids((8, 128))
        for half in range(2):
            for t in range(HALF // 8):
                shift = (8 * t) % 128
                x, z = diag_ref[2 * half, n], diag_ref[2 * half + 1, n]
                if 8 * t >= 128:
                    x, z = z, x
                if shift:
                    x, z = pltpu.roll(x, shift, 1), pltpu.roll(z, shift, 1)
                    x, z = jnp.where(lanes >= shift, x, z), jnp.where(lanes >= shift, z, x)
                rows = pl.ds(8 * t, 8)
                bias_ref[n, half, 0, rows] = x
                bias_ref[n, half, 1, rows] = z
        return carry

    lax.fori_loop(0, 16, spread, 0)
    tok_load.wait()

    def load_pair(pair):
        rows = load_ref[pl.ds(pair * pair_rows, pair_rows)].astype(F32)
        for n in range(2):
            one = rows[n * PIX : n * PIX + PIX]
            nat_ref[0, 2 * pair + n] = jnp.concatenate([one, jnp.zeros((8, 256), F32)], axis=0).astype(BF16)

    def late_start():
        head_of_row = lax.broadcasted_iota(jnp.int32, (256, 1024), 0) // HEAD
        head_of_lane = lane_ids((256, 1024)) // 128
        ones_ref[...] = jnp.where(head_of_row == head_of_lane, 1.0, 0.0).astype(BF16)
        diag_ref[...] = jnp.zeros_like(diag_ref)
        gs_ref[...] = jnp.zeros_like(gs_ref)
        wide_acc[...] = jnp.zeros_like(wide_acc)
        slim_acc[...] = jnp.zeros_like(slim_acc)
        for pair in range(1, images // 2):
            load_pair(pair)

    load_pair(0)
    pl.when(block == 1)(late_start)
    for copy in constants:
        copy.wait()
    await_bytes(small_ref.at[0], small_sems.at[1])
    await_bytes(win_ref.at[0], win_sems.at[1])

    def spacing(i):
        return jnp.maximum(dil_ref[block, first + i] - 1, 0)

    def mask_for(i):
        d = spacing(i)
        rows_valid = mask_ref[first + i, 0]
        for r in range(1, R_SIDE):
            rows_valid = rows_valid + mask_ref[first + i, r * C_SIDE]
        cols_valid = mask_ref[first + i, 0]
        for c in range(1, C_SIDE):
            cols_valid = cols_valid + mask_ref[first + i, c]
        for half in range(2):
            allowed = (lrow_ref[d, half] < rows_valid) & (lcol_ref[d, half] < cols_valid)
            shut = jnp.where(allowed, 0.0, NEG)[0:1]
            maskadd_ref[half] = window_ref[d, half].astype(F32) + shut

    def give_copies(kind, pair):
        target = pl.ds(pl.multiple_of(core * rows_own + pair * pair_rows, 16), pair_rows)
        target = (out_hbm, back_hbm)[kind // 2].at[0, target]
        source = give_ref.at[kind, pair, pl.ds(0, pair_rows)]
        recv = give_recv.at[kind // 2]
        remote = mesh_copy(source, target, give_send.at[kind, pair], recv, sibling, me)
        local = pltpu.make_async_copy(source, target, recv)
        return remote, local

    def cross_copy(i):
        return mesh_copy(nat_ref.at[0, i], nat_ref.at[1, i], cross_send.at[i], cross_recv.at[i], across, me)

    def record(kind, i, low):
        give_ref[kind, lax.div(i, 2), pl.ds(pl.multiple_of(lax.rem(i, 2) * PAD, 16), PAD)] = low

    def cross(kind, i):
        low = give_ref[kind, lax.div(i, 2), pl.ds(pl.multiple_of(lax.rem(i, 2) * PAD, 16), PAD)]
        nat_ref[0, i] = dot_nn(permt_ref[spacing(i)], low).astype(BF16)
        cross_copy(i).start()

    def await_cross(i):
        await_bytes(nat_ref.at[1, i], cross_recv.at[i])

    def deliver(kind, pair):
        rows = []
        for n in range(2):
            low = give_ref[kind, pair, n * PAD : n * PAD + PAD]
            rows.append(dot_nn(permt_ref[spacing(2 * pair + n)], low)[0:PIX])
        give_ref[kind, pair, 0:pair_rows] = jnp.concatenate(rows, axis=0).astype(BF16)
        remote, local = give_copies(kind, pair)
        pl.when(core != kind % 2)(remote.start)
        pl.when(core == kind % 2)(local.start)

    def deliver_all(kind, start):
        def one(pair, carry):
            deliver(kind, pair)
            return carry

        lax.fori_loop(start, images // 2, one, 0)

    def forward(i):
        d = spacing(i)
        turn = turn_ref[first + i]
        mask_for(i)
        x = dot_nn(perm_ref[d], nat_ref[block, i])
        xhat, rstd = normalise(x)
        xhat_ref[0, i] = xhat
        rstd_ref[0, i] = rstd
        normed = (xhat * small_ref[0, 0:1] + small_ref[0, 1:2]).astype(BF16)
        mixed = dot_nn(normed, win_ref[0])
        scaled = (mixed[:, 0:256] + small_ref[0, 3:4]) * (HEAD**-0.5 * LOG2E)
        qkv_ref[i, :, 0:256] = scaled.astype(BF16)
        qkv_ref[i, :, 256:512] = (mixed[:, 256:512] + small_ref[0, 4:5]).astype(BF16)
        qkv_ref[i, :, 512:768] = (mixed[:, 512:768] + small_ref[0, 5:6]).astype(BF16)
        ones = jnp.ones((256, 128), BF16)
        attended = []
        inverse = []
        for half in range(2):
            yield True
            query = scaled[QUERY_AT[half] : QUERY_AT[half] + HALF].astype(BF16)
            key_rows = pl.ds(KEY_AT[half], 256)
            scores = dot_nt(mask_heads(query), qkv_ref[i, key_rows, 256:512])
            for h in range(HEADS):
                n = turn * 8 + h
                part = scores[h * HALF : (h + 1) * HALF]
                left = part[:, 0:128] + (bias_ref[n, half, 0] + maskadd_ref[half, :, 0:128])
                right = part[:, 128:256] + (bias_ref[n, half, 1] + maskadd_ref[half, :, 128:256])
                top = jnp.max(jnp.maximum(left, right), axis=-1, keepdims=True)
                rows = pl.ds(h * HALF, HALF)
                prob_ref[i, half, rows, 0:128] = jnp.exp2(left - top).astype(BF16)
                prob_ref[i, half, rows, 128:256] = jnp.exp2(right - top).astype(BF16)
            yield True
            values = []
            inverses = []
            for part in range(2):
                right = jnp.concatenate([qkv_ref[i, key_rows, 512 + part * 128 : 640 + part * 128], ones], axis=1)
                stack = dot_nn(prob_ref[i, half, pl.ds(part * 4 * HALF, 4 * HALF)], right)
                inverses.append(1.0 / pick_heads(stack[:, 128:256]))
                values.append(pick_heads(stack[:, 0:128]) * inverses[part])
            attended.append(jnp.concatenate(values, axis=1))
            inverse.append(jnp.where(lane_ids((HALF, 128)) % HEAD < 16, inverses[0], inverses[1]))
        att_ref[i] = join_halves(*attended).astype(BF16)
        inverse_ref[i] = join_halves(*inverse)
        y = (x + dot_nn(att_ref[i], proj_ref[...]) + small_ref[0, 2:3]).astype(BF16)
        record(0, i, y)
        yield True
        x = y.astype(F32)
        xhat, rstd = normalise(x)
        xhat_ref[1, i] = xhat
        rstd_ref[1, i] = rstd
        normed = (xhat * small_ref[1, 0:1] + small_ref[1, 1:2]).astype(BF16)
        for part in range(3):
            yield True
            cols = slice(part * 256, part * 256 + 256)
            hidden = dot_nn(normed, win_ref[1, :, cols]) + small_ref[1, 3 + part : 4 + part]
            active, slope = gelu_pair(hidden)
            act_ref[i, :, cols] = active.astype(BF16)
            slope_ref[i, :, cols] = slope.astype(BF16)
        yield True
        z = (x + dot_nn(act_ref[i], down_ref[...]) + small_ref[1, 2:3]).astype(BF16)
        record(1, i, z)

    def norm_backward(i, t, g, dmix):
        dn = dot_nt(dmix, win_ref[t])
        xhat = xhat_ref[t, i]
        gs_ref[t, 0:1] += jnp.sum(dn * xhat, axis=0, keepdims=True)
        gs_ref[t, 1:2] += jnp.sum(dn, axis=0, keepdims=True)
        gs_ref[t, 2:3] += jnp.sum(g, axis=0, keepdims=True)
        e = dn * small_ref[t, 0:1]
        first_mean = jnp.mean(e, axis=-1, keepdims=True)
        second_mean = jnp.mean(e * xhat, axis=-1, keepdims=True)
        return (g + (e - first_mean - xhat * second_mean) * rstd_ref[t, i]).astype(BF16)

    def feed_backward(i):
        g = dot_nn(perm_ref[spacing(i)], nat_ref[1 - block, i])
        low = g.astype(BF16)
        nat_ref[1, i] = low
        for part in range(3):
            yield True
            cols = slice(part * 256, part * 256 + 256)
            dact = dot_nt(low, down_ref[cols])
            dhidden = dact * slope_ref[i, :, cols].astype(F32)
            gs_ref[1, 3 + part : 4 + part] += jnp.sum(dhidden, axis=0, keepdims=True)
            slope_ref[i, :, cols] = dhidden.astype(BF16)
        yield True
        result = norm_backward(i, 1, g, slope_ref[i])
        up_ref[i] = result
        record(3, i, result)

    def attention_backward(i):
        turn = turn_ref[first + i].astype(F32)
        low = up_ref[i]
        packed = inverse_ref[i]
        lanes = lane_ids(packed.shape) % HEAD
        inverse = jnp.concatenate(
            [
                jnp.where(lanes < 16, packed, pltpu.roll(packed, 16, 1)),
                jnp.where(lanes < 16, pltpu.roll(packed, 112, 1), packed),
            ],
            axis=1,
        )
        datt_all = dot_nt(low, proj_ref[...]) * inverse
        attended = att_ref[i].astype(F32)
        query_all = qkv_ref[i, :, 0:256].astype(F32)
        dqueries = []
        dkvs = []
        for half in range(2):
            yield True
            rows_half = slice(QUERY_AT[half], QUERY_AT[half] + HALF)
            key_rows = pl.ds(KEY_AT[half], 256)
            datt32 = own_rows(datt_all[rows_half], half)
            datt = datt32.astype(BF16)
            query_t = query_all[rows_half].astype(BF16).T
            datt_t = datt.T
            dprob = dot_nt(mask_heads(datt), qkv_ref[i, key_rows, 512:768])
            totals = dot_nn((datt32 * attended[rows_half]).astype(BF16), ones_ref[...])
            dkeys = []
            dvalues = []
            ds = []
            for h in range(HEADS):
                rows = pl.ds(h * HALF, HALF)
                prob = prob_ref[i, half, rows]
                total = totals[:, h * 128 : h * 128 + 128]
                part = dprob[h * HALF : (h + 1) * HALF]
                left = prob[:, 0:128].astype(F32) * (part[:, 0:128] - total)
                right = prob[:, 128:256].astype(F32) * (part[:, 128:256] - total)
                for kind, value in enumerate(diagonal_sums(left, right)):
                    diag_ref[2 * half + kind, h] += value * (1.0 - turn)
                    diag_ref[2 * half + kind, 8 + h] += value * turn
                ds.append(jnp.concatenate([left.astype(BF16), right.astype(BF16)], axis=1))
                head_rows = slice(h * HEAD, (h + 1) * HEAD)
                dkeys.append(dot_nn(query_t[head_rows], ds[h]))
                dvalues.append(dot_nn(datt_t[head_rows], prob))
            parts = []
            for part in range(2):
                keys = qkv_ref[i, key_rows, 256 + part * 128 : 384 + part * 128]
                parts.append(pick_heads(dot_nn(jnp.concatenate(ds[4 * part : 4 * part + 4], axis=0), keys)))
            dqueries.append(jnp.concatenate(parts, axis=1))
            yield True
            dkeys = jnp.concatenate(dkeys, axis=0).T * LN2
            dvalues = jnp.concatenate(dvalues, axis=0).T
            dkvs.append(jnp.concatenate([dkeys, dvalues], axis=1))
        yield True
        dquery = join_halves(*dqueries) * HEAD**-0.5
        dkv = jnp.concatenate([dkvs[0][0:32], dkvs[0][32:256] + dkvs[1][0:224], dkvs[1][224:256]], axis=0)
        gs_ref[0, 3:4] += jnp.sum(dquery, axis=0, keepdims=True)
        gs_ref[0, 4:5] += jnp.sum(dkv[:, 0:256], axis=0, keepdims=True)
        gs_ref[0, 5:6] += jnp.sum(dkv[:, 256:512], axis=0, keepdims=True)
        qkv_ref[i, :, 0:256] = dquery.astype(BF16)
        qkv_ref[i, :, 256:768] = dkv.astype(BF16)
        yield True
        result = norm_backward(i, 0, low.astype(F32), qkv_ref[i])
        record(2, i, result)

    def early_sides():
        slim.start_side(0)
        wide.start_side(0)

    def add_in(t, at, count):
        rows = count * PAD
        dmix = (qkv_ref, slope_ref)[t][pl.ds(at, count)].reshape(rows, 768)
        xhat = xhat_ref[t, pl.ds(at, count)].reshape(rows, 256)
        normed = (xhat * small_ref[t, 0:1] + small_ref[t, 1:2]).astype(BF16)
        wide_acc[t] += dot_tn(normed, dmix)

    def add_feed(at, count):
        rows = count * PAD
        up = nat_ref[1, pl.ds(at, count)].reshape(rows, 256)
        for part in range(3):
            cols = slice(part * 256, part * 256 + 256)
            slim_acc[0, :, cols] += dot_tn(act_ref[pl.ds(at, count), :, cols].reshape(rows, 256), up)
        add_in(1, at, count)
        after = up_ref[pl.ds(at, count)].reshape(rows, 256)
        slim_acc[0, :, 768:1024] += dot_tn(att_ref[pl.ds(at, count)].reshape(rows, 256), after)

    def start_feed():
        slim.start_core(0)
        wide.start_core(0)

    def backward(i):
        yield from feed_backward(i)
        yield from attention_backward(i)

    def feed_and_sums(i):
        yield from feed_backward(i)
        yield True
        add_feed(i, 1)

    def attention_and_sums(i):
        yield from attention_backward(i)
        yield True
        add_in(0, i, 1)

    def over(start, stop, work):
        def one(i, carry):
            work(i)
            return carry

        lax.fori_loop(start, stop, one, 0)

    def first_forward(i):
        pl.when(block == 1)(lambda: await_cross(i))
        together(forward(i))

        @pl.when(block == 0)
        def _():
            cross(1, i)
            pl.when(i == 0)(late_start)

            @pl.when(lax.rem(i, 2) == 1)
            def _():
                deliver(0, lax.div(i, 2))
                deliver(1, lax.div(i, 2))

    over(0, jnp.where(block == 0, images, 1), first_forward)

    def back_and_forth(i):
        await_cross(i + 1)
        together(backward(i), forward(i + 1))
        cross(2, i)

    over(0, jnp.where(block == 0, 0, images - 1), back_and_forth)

    def early_feed(i):
        await_cross(i)
        together(feed_and_sums(i))

        @pl.when(lax.rem(i, 2) == 1)
        def _():
            pl.when(i < images - 1)(lambda: deliver(3, lax.div(i, 2)))

    over(0, jnp.where(block == 0, LAG, 0), early_feed)

    def both_backward(i):
        await_cross(i)
        together(feed_and_sums(i), attention_and_sums(i - LAG))
        pl.when(lax.rem(i, 2) == 1)(lambda: deliver(3, lax.div(i, 2)))
        pl.when((lax.rem(i, 2) == 1) & (i >= 3))(lambda: deliver(2, lax.div(i - 3, 2)))

    over(LAG, jnp.where(block == 0, images - 1, LAG), both_backward)
    over(jnp.where(block == 0, images - 1, images), images, early_feed)

    @pl.when(block == 0)
    def _():
        start_feed()
        deliver(3, images // 2 - 1)
        deliver(2, images // 2 - 2)
        early_sides()
        together(attention_and_sums(images - 2), attention_and_sums(images - 1))
        slim.start_cut(0)

    @pl.when(block == 1)
    def _():
        together(backward(images - 1))
        cross(2, images - 1)
        over(0, images // 4, lambda n: add_feed(4 * n, 4))
        start_feed()
        over(0, images // 4, lambda n: add_in(0, 4 * n, 4))
        early_sides()
        tall.start_core()
        deliver_all(3, 0)
        slim.start_cut(0)
        deliver_all(0, 0)

    piece_rows = pl.ds(pl.multiple_of(pair_of * 16, 16), 16)
    quarter_rows = pl.ds(pl.multiple_of(128 * core + 64 * side + 16 * pair_of, 16), 16)
    far = block == 0
    pl.when(block == 0)(tall.start_core)
    wide.start_cut(0)

    table_sum = jnp.zeros((8, 256), F32)
    for turn in range(2):
        rows = pl.ds(turn * 8, 8)
        sums = []
        for half in range(2):
            total = jnp.zeros((8, 256), F32)
            for s in range(8):
                ring = jnp.concatenate([diag_ref[2 * half, rows, s], diag_ref[2 * half + 1, rows, s]], axis=1)
                total = total + (pltpu.roll(ring, 256 - s, 1) if s else ring)
            sums.append(total)
        sums = jnp.concatenate(sums, axis=1)
        upper = sums.astype(BF16)
        lower = (sums - upper.astype(F32)).astype(BF16)
        table_sum = table_sum + dot_nt(upper, pick_ref[turn]) + dot_nt(lower, pick_ref[turn])

    note_send[0:8] = gs_ref[1 - core]
    note_send[8:16] = table_sum
    note_core[core, 0:8] = gs_ref[core]
    note_core[core, 8:16] = table_sum
    note_copy = mesh_copy(note_send, note_core.at[core], note_sems.at[0], note_sems.at[1], sibling, me)
    note_copy.start()
    tall.start_cut()
    slim.sum_pieces(0)
    slim.start_gather(0, land_down.at[block, core, side, piece_rows], land_sems.at[1, block], p, far)
    wide.sum_pieces(0)
    wide.start_gather(0, land_in.at[quarter_rows], land_sems.at[0, 1], 2 * block + 1)
    note_copy.wait_recv()
    note_side[side] = note_core[0] + note_core[1]
    side_copy = mesh_copy(note_side.at[side], note_side.at[side], note_sems.at[2], note_sems.at[3], p, partner)
    side_copy.start()

    def side_share(b):
        land = land_down.at[b, core, side]
        return mesh_copy(land, land, side_send.at[0, b], side_recv.at[0, b], p, partner)

    def side_start(b):
        await_bytes(land_down.at[b, 0, 0], land_sems.at[1, b])
        side_share(b).start()

    side_start(block)
    deliver_all(2, jnp.where(block == 0, LATE_PAIR, 0))
    deliver_all(1, jnp.where(block == 0, images // 2, 0))
    side_copy.wait_recv()
    note_all[pair_of] = note_side[0] + note_side[1]

    def send_note(j, carry):
        @pl.when(j != pair_of)
        def _():
            place = note_all.at[pair_of]
            mesh_copy(place, place, note_sems.at[4], note_sems.at[5], p, 2 * j + side).start()

        return carry

    lax.fori_loop(0, dp // 2, send_note, 0)

    def share_copy(b):
        land = land_down.at[b, core]
        return mesh_copy(land, land, share_send.at[b], share_recv.at[b], sibling, me)

    tall.start_gather(land_in, land_sems.at[0, 0])
    def cross_share():
        land = land_down.at[1, core]
        return mesh_copy(land, land, far_send, far_recv, across, me)

    side_share(block).wait_recv()
    share_copy(block).start()
    pl.when(block == 1)(lambda: cross_share().start())
    await_bytes(note_all.at[pl.ds(0, dp // 2 - 1)], note_sems.at[5])

    def add_note(j, total):
        return total + note_all[j]

    notes = lax.fori_loop(0, dp // 2, add_note, jnp.zeros((16, 256), F32))
    notes_ref[0] = notes[0:8]
    note_far[0] = notes[8:16]
    far_copy = mesh_copy(note_far.at[0], note_far.at[1], note_sems.at[6], note_sems.at[7], across, me)
    far_copy.start()

    def in_copies():
        copies = []
        for c in range(2):
            rows = land_in.at[pl.ds(pl.multiple_of(128 * c + 64 * side, 64), 64)]
            copies.append(mesh_copy(rows, rows, side_send.at[2, c], side_recv.at[2, c], p, partner))
        return copies

    @pl.when(core == 1)
    def _():
        await_bytes(land_in.at[0:128], land_sems.at[0, 1])
        for copy in in_copies():
            copy.start()

    @pl.when(block == 1)
    def _():
        side_start(0)
        side_share(0).wait_recv()

    pl.when(block == 0)(lambda: cross_share().wait_recv())
    share_copy(1 - block).start()
    far_copy.wait_recv()
    notes_ref[1 + block] = note_far[0]
    notes_ref[2 - block] = note_far[1]
    notes_copy = pltpu.make_async_copy(notes_ref, notes_hbm, load_sem.at[4])
    notes_copy.start()

    pl.when(core == 0)(lambda: await_bytes(land_in, land_sems.at[0, 0]))

    @pl.when(core == 1)
    def _():
        for copy in in_copies():
            copy.wait()

    results = [notes_copy, pltpu.make_async_copy(land_in, sum_in_hbm, load_sem.at[0])]
    results[1].start()
    for b in (1, 0):
        share_copy(b).wait()
        results.append(pltpu.make_async_copy(land_down.at[b], sum_down_hbm.at[b], load_sem.at[2 + b]))
        results[-1].start()
    await_bytes(out_hbm, give_recv.at[0])
    await_bytes(back_hbm, give_recv.at[1])
    for kind in range(4):

        @pl.when(core != kind % 2)
        def _(kind=kind):
            for pair in range(images // 2):
                give_copies(kind, pair)[0].wait_send()

    for i in range(images):
        cross_copy(i).wait_send()
    win_copy.wait_send()
    small_copy.wait_send()
    note_copy.wait_send()
    side_copy.wait_send()
    far_copy.wait_send()
    await_bytes(note_all.at[pl.ds(0, dp // 2 - 1)], note_sems.at[4])
    side_share(block).wait_send()

    @pl.when(block == 1)
    def _():
        side_share(0).wait_send()
        cross_share().wait_send()

    for copy in results:
        copy.wait()
    tall.finish_sends()
    wide.finish_sends(0, 2 * block + 1)
    slim.finish_sends(0, p, far)


def result_kernel(
    out_raw,
    back_raw,
    sum_in,
    sum_down,
    notes_hbm,
    out_hbm,
    back_hbm,
    g_in_hbm,
    g_proj_hbm,
    g_down_hbm,
    g_gain_hbm,
    g_shift_hbm,
    g_bin_hbm,
    g_bout_hbm,
    g_table_hbm,
    out_buf,
    back_buf,
    in_buf,
    down_buf,
    notes,
    g_in,
    g_proj,
    g_down,
    g_gain,
    g_shift,
    g_bin,
    g_bout,
    g_table,
    load_sems,
    store_sems,
    part_sems,
):
    low = [(notes_hbm, notes), (sum_in, in_buf), (sum_down, down_buf)]
    sums = [pltpu.make_async_copy(source, target, load_sems.at[n]) for n, (source, target) in enumerate(low)]
    rows = out_buf.shape[0] // 4
    loads = []
    stores = []
    for part in range(4):
        at = pl.ds(part * rows, rows)
        for n, (raw, buf, target) in enumerate(((out_raw, out_buf, out_hbm), (back_raw, back_buf, back_hbm))):
            loads.append(pltpu.make_async_copy(raw.at[0, at], buf.at[at], part_sems.at[0, n, part]))
            stores.append(pltpu.make_async_copy(buf.at[at], target.at[0, at], part_sems.at[1, n, part]))
    for copy in sums + loads:
        copy.start()
    full = [
        (g_gain, g_gain_hbm),
        (g_shift, g_shift_hbm),
        (g_bin, g_bin_hbm),
        (g_bout, g_bout_hbm),
        (g_table, g_table_hbm),
        (g_in, g_in_hbm.at[0]),
        (g_proj, g_proj_hbm),
        (g_down, g_down_hbm),
    ]
    finals = [pltpu.make_async_copy(source, target, store_sems.at[n]) for n, (source, target) in enumerate(full)]
    sums[0].wait()
    g_gain[...] = notes[0, 0:1]
    g_shift[...] = notes[0, 1:2]
    g_bout[...] = notes[0, 2:3]
    for part in range(3):
        cols = slice(part * 256, part * 256 + 256)
        g_bin[:, cols] = notes[0, 3 + part : 4 + part]
    for b in range(2):
        g_table[b] = notes[1 + b, :, 0 : SPAN * SPAN]
    for copy in finals[0:5]:
        copy.start()
    sums[1].wait()
    g_in[...] = in_buf[...].astype(F32)
    finals[5].start()
    sums[2].wait()
    for b in range(2):
        g_proj[b] = down_buf[b, :, :, :, 768:1024].reshape(256, 256).astype(F32)
        for part in range(3):
            cols = slice(part * 256, part * 256 + 256)
            g_down[b, cols] = down_buf[b, :, :, :, cols].reshape(256, 256).astype(F32)
    finals[6].start()
    finals[7].start()
    for load, store in zip(loads, stores):
        load.wait()
        store.start()
    for store in finals + stores:
        store.wait()


def run_kernels(dp, images, smem_operands, hbm_operands, vmem_operands):
    tables = [jnp.asarray(t) for t in constant_tables()]
    rows = images * PIX
    vmem = pl.BlockSpec(memory_space=pltpu.VMEM)
    smem = pl.BlockSpec(memory_space=pltpu.SMEM)
    hbm = pl.BlockSpec(memory_space=pl.ANY)
    dma = pltpu.SemaphoreType.DMA
    raw_shape = (
        jax.ShapeDtypeStruct((1, 2 * rows, 256), BF16),
        jax.ShapeDtypeStruct((1, 2 * rows, 256), BF16),
        jax.ShapeDtypeStruct((256, 768), BF16),
        jax.ShapeDtypeStruct((2, 2, 2, 64, 1024), BF16),
        jax.ShapeDtypeStruct((3, 8, 256), F32),
    )
    out_shape = raw_shape[0:2] + (
        jax.ShapeDtypeStruct((1, 256, 768), F32),
        jax.ShapeDtypeStruct((2, 256, 256), F32),
        jax.ShapeDtypeStruct((2, 768, 256), F32),
        jax.ShapeDtypeStruct((1, 256), F32),
        jax.ShapeDtypeStruct((1, 256), F32),
        jax.ShapeDtypeStruct((1, 768), F32),
        jax.ShapeDtypeStruct((1, 256), F32),
        jax.ShapeDtypeStruct((2, HEADS, SPAN * SPAN), F32),
    )

    def pack(sums, count, columns):
        return [
            pltpu.VMEM((sums, 256, columns), F32),
            pltpu.VMEM((count, 256, columns), BF16),
            pltpu.VMEM((count, 128, columns), BF16),
            pltpu.VMEM((count, 64, columns), BF16),
            pltpu.VMEM((count, 4, 16, columns), BF16),
            pltpu.VMEM((count, dp // 2, 16, columns), BF16),
            pltpu.VMEM((count, 16, columns), BF16),
        ]

    scratch = [
        *[pltpu.VMEM(shape.shape, shape.dtype) for shape in raw_shape[2:5]],
        pltpu.VMEM((256, 256), BF16),
        pltpu.VMEM((768, 256), BF16),
        *[pltpu.VMEM(table.shape, table.dtype) for table in tables],
        pltpu.VMEM((2, images, PAD, 256), BF16),
        pltpu.VMEM((2, images, PAD, 256), F32),
        pltpu.VMEM((2, images, PAD, 1), F32),
        pltpu.VMEM((images, PAD, 768), BF16),
        pltpu.VMEM((images, 2, HEADS * HALF, 256), BF16),
        pltpu.VMEM((images, PAD, 256), BF16),
        pltpu.VMEM((images, PAD, 768), BF16),
        pltpu.VMEM((images, PAD, 768), BF16),
        pltpu.VMEM((images, PAD, 256), BF16),
        pltpu.VMEM((images, PAD, 128), F32),
        pltpu.VMEM((256, 1024), BF16),
        pltpu.VMEM((2, HALF, 256), F32),
        pltpu.VMEM((16, 2, 2, HALF, 128), F32),
        pltpu.VMEM((8, 256), F32),
        pltpu.VMEM((4, 16, 8, 128), F32),
        pltpu.VMEM((2, 256, 768), BF16),
        pltpu.VMEM((2, 8, 256), F32),
        pltpu.VMEM((2, 8, 256), F32),
        pltpu.VMEM((4, images // 2, 2 * PAD, 256), BF16),
        pltpu.VMEM((rows, 256), BF16),
        *pack(2, 1, 768),
        *pack(1, 1, 1024),
        pltpu.VMEM((256, 768), BF16),
        pltpu.VMEM((128, 768), BF16),
        pltpu.VMEM((8, 16, 768), BF16),
        pltpu.VMEM((dp, 16, 768), BF16),
        pltpu.VMEM((16, 768), BF16),
        pltpu.VMEM((16, 256), F32),
        pltpu.VMEM((2, 16, 256), F32),
        pltpu.VMEM((2, 16, 256), F32),
        pltpu.VMEM((dp // 2, 16, 256), F32),
        pltpu.VMEM((2, 8, 256), F32),
        dma((6,)),
        dma((8,)),
        dma((2,)),
        dma((2,)),
        dma((4, images // 2)),
        dma((2,)),
        dma((images,)),
        dma((images,)),
        dma((8, 1)),
        dma((8, 1)),
        dma((5,)),
        dma((3, 2)),
        dma((2,)),
        dma((2,)),
        dma((3, 2)),
        dma((3, 2)),
        dma,
        dma,
        dma((8,)),
    ]
    raw = pl.pallas_call(
        functools.partial(section_kernel, images, dp),
        out_shape=raw_shape,
        in_specs=[smem] * 3 + [hbm] * 3 + [vmem] * 5 + [hbm] * 8,
        out_specs=[hbm] * 5,
        scratch_shapes=scratch,
        compiler_params=pltpu.CompilerParams(
            vmem_limit_bytes=63 * 1024 * 1024, collective_id=0, has_side_effects=True
        ),
    )(*smem_operands, *hbm_operands, *vmem_operands, *tables)
    return pl.pallas_call(
        result_kernel,
        out_shape=out_shape,
        in_specs=[hbm] * 5,
        out_specs=[hbm] * 10,
        scratch_shapes=[
            pltpu.VMEM((2 * rows, 256), BF16),
            pltpu.VMEM((2 * rows, 256), BF16),
            *[pltpu.VMEM(shape.shape, shape.dtype) for shape in raw_shape[2:5]],
            pltpu.VMEM((256, 768), F32),
            *[pltpu.VMEM(shape.shape, F32) for shape in out_shape[3:10]],
            dma((3,)),
            dma((8,)),
            dma((2, 2, 4)),
        ],
        compiler_params=pltpu.CompilerParams(vmem_limit_bytes=63 * 1024 * 1024),
    )(*raw)


def body(
    tokens_in,
    cotangent,
    valid_mask,
    orientation,
    dilation,
    norm_gain,
    norm_bias,
    in_weight,
    in_bias,
    out_bias,
    proj_weight,
    down_weight,
    position_bias,
):
    images = valid_mask.shape[0] // 2
    results = run_kernels(
        lax.axis_size("dp"),
        images,
        (valid_mask, orientation, dilation.T),
        (tokens_in, cotangent, in_weight),
        (norm_gain, norm_bias, in_bias, out_bias, position_bias, proj_weight, down_weight),
    )
    out, back, g_in, g_proj, g_down, g_gain, g_shift, g_bin, g_bout, g_table = results
    return out, back, g_gain, g_shift, g_in, g_bin, g_bout, g_proj, g_down, g_table


def solution(mesh):
    placed = (
        P("dp", None),
        P("dp", None),
        P("dp", None),
        P("dp"),
        P("dp", None),
        P("pipe", None),
        P("pipe", None),
        P("pipe", None, None),
        P("pipe", None),
        P("pipe", None),
        P(),
        P(),
        P(),
    )
    return jax.shard_map(
        body,
        mesh=mesh,
        in_specs=placed,
        out_specs=(
            P("pipe", "dp", None),
            P("pipe", "dp", None),
            P("pipe", None),
            P("pipe", None),
            P("pipe", None, None),
            P("pipe", None),
            P("pipe", None),
            P(),
            P(),
            P(),
        ),
        check_vma=False,
    )
```

```python
import functools
import math

import jax
import jax.numpy as jnp
import ml_dtypes
import numpy as np
from jax import lax
from jax.experimental import pallas as pl
from jax.experimental.pallas import tpu as pltpu
from jax.sharding import PartitionSpec as P

HEADS = 8
HEAD = 32
KS = 7
R_SIDE = 14
C_SIDE = 20
PIX = 280
SPAN = 13
EPS = 1e-05
NEG = -1e30
HALF = 144
PAD = 288
OWN = 140
LAG = 1
LATE_PAIR = 3
QUERY_AT = (0, 136)
KEY_AT = (0, 32)
LOG2E = math.log2(math.e)
LN2 = math.log(2.0)
F32 = jnp.float32
BF16 = jnp.bfloat16


def token_places(dilation):
    place = np.arange(PIX)
    if dilation == 1:
        return place // C_SIDE, place % C_SIDE
    row_class, rest = place // OWN, place % OWN
    row_local, rest = rest // C_SIDE, rest % C_SIDE
    col_class, col_local = rest // 10, rest % 10
    return row_local * 2 + row_class, col_local * 2 + col_class


def line_window(q, k, dilation, length):
    same = (q % dilation) == (k % dilation)
    count = (length - q % dilation + dilation - 1) // dilation
    start = np.clip(q // dilation - KS // 2, 0, count - KS)
    reach = k // dilation - start
    return same & (reach >= 0) & (reach < KS)


def constant_tables():
    window = np.zeros((2, 2, HALF, 256), np.float32)
    lane_row = np.full((2, 2, 8, 256), 1000, np.int32)
    lane_col = np.full((2, 2, 8, 256), 1000, np.int32)
    perm = np.zeros((2, PAD, PAD), np.float32)
    for d in (1, 2):
        rows, cols = token_places(d)
        perm[d - 1, np.arange(PIX), rows * C_SIDE + cols] = 1
        for half in (0, 1):
            keys = KEY_AT[half] + np.arange(256)
            real = keys < PIX
            key_row = np.where(real, rows[np.minimum(keys, PIX - 1)], 1000)
            key_col = np.where(real, cols[np.minimum(keys, PIX - 1)], 1000)
            query = half * OWN + np.arange(OWN)
            inside = (
                line_window(rows[query][:, None], key_row[None], d, R_SIDE)
                & line_window(cols[query][:, None], key_col[None], d, C_SIDE)
                & real[None]
            )
            window[d - 1, half, query - QUERY_AT[half]] = np.where(inside, 0.0, NEG)
            lane_row[d - 1, half] = key_row[None]
            lane_col[d - 1, half] = key_col[None]
    pick = np.zeros((2, 256, 512), np.float32)
    for m in range(-6, 7):
        for w in range(-6, 7):
            gap = 20 * m + w
            for turn in (0, 1):
                entry = (m + 6) * SPAN + w + 6 if turn == 0 else (w + 6) * SPAN + m + 6
                for half in (0, 1):
                    pick[turn, entry, half * 256 + (gap + QUERY_AT[half] - KEY_AT[half]) % 256] = 1
    low = ml_dtypes.bfloat16
    return (
        window.astype(low),
        lane_row,
        lane_col,
        perm.astype(low),
        perm.transpose(0, 2, 1).astype(low),
        pick.astype(low),
    )


def dot_nn(a, b):
    return lax.dot_general(a, b, (((1,), (0,)), ((), ())), preferred_element_type=F32)


def dot_nt(a, b):
    return lax.dot_general(a, b, (((1,), (1,)), ((), ())), preferred_element_type=F32)


def dot_tn(a, b):
    return lax.dot_general(a, b, (((0,), (0,)), ((), ())), preferred_element_type=F32)


def lane_ids(shape):
    return lax.broadcasted_iota(jnp.int32, shape, len(shape) - 1)


def normalise(x):
    center = x - jnp.mean(x, axis=-1, keepdims=True)
    rstd = lax.rsqrt(jnp.mean(center * center, axis=-1, keepdims=True) + EPS)
    return center * rstd, rstd


def gelu_pair(h):
    phi = 0.5 + 0.5 * lax.erf(h * math.sqrt(0.5))
    e = jnp.exp2(h * h * (-0.5 * LOG2E))
    return h * phi, phi + h * (e * (1.0 / math.sqrt(2.0 * math.pi)))


def mask_heads(rows):
    lanes = lane_ids((1, 256)) // HEAD
    return jnp.concatenate([rows * jnp.where(lanes == h, 1.0, 0.0).astype(BF16) for h in range(HEADS)], axis=0)


def pick_heads(stack):
    lanes = lane_ids((HALF, 128)) // HEAD
    total = stack[0:HALF]
    for h in range(1, 4):
        total = jnp.where(lanes == h, stack[h * HALF : (h + 1) * HALF], total)
    return total


def diagonal_sums(left, right):
    lanes = lane_ids((8, 128))
    low = jnp.zeros((8, 128), F32)
    high = jnp.zeros((8, 128), F32)
    for t in range(HALF // 8):
        shift = (8 * t) % 128
        a = left[8 * t : 8 * t + 8]
        b = right[8 * t : 8 * t + 8]
        if 8 * t >= 128:
            a, b = b, a
        if shift:
            a = pltpu.roll(a, 128 - shift, 1)
            b = pltpu.roll(b, 128 - shift, 1)
            near = lanes < 128 - shift
            a, b = jnp.where(near, a, b), jnp.where(near, b, a)
        low = low + a
        high = high + b
    return low, high


def together(*works):
    works = list(works)
    while works:
        for work in list(works):
            if next(work, None) is None:
                works.remove(work)


def join_halves(first, second):
    upper = lax.broadcasted_iota(jnp.int32, (8, first.shape[1]), 0) < 4
    seam = jnp.where(upper, first[136:144], second[0:8])
    tail = jnp.zeros((8, first.shape[1]), first.dtype)
    return jnp.concatenate([first[0:136], seam, second[8:144], tail], axis=0)


def own_rows(rows, half):
    upper = lax.broadcasted_iota(jnp.int32, (8, rows.shape[1]), 0) < 4
    if half == 0:
        return jnp.concatenate([rows[0:136], jnp.where(upper, rows[136:144], 0.0)], axis=0)
    return jnp.concatenate([jnp.where(upper, 0.0, rows[0:8]), rows[8:144]], axis=0)


def mesh_copy(src, dst, send, recv, pipe, dp):
    return pltpu.make_async_remote_copy(
        src_ref=src,
        dst_ref=dst,
        send_sem=send,
        recv_sem=recv,
        device_id=(pipe, dp),
        device_id_type=pl.DeviceIdType.MESH,
    )


def await_bytes(like, sem):
    pltpu.make_async_copy(like, like, sem).wait()


class Pack:
    def __init__(self, dp, refs, sems):
        self.pairs = dp // 2
        self.acc, self.send, self.core, self.side, self.cut, self.gather, self.total = refs
        self.core_send, self.core_recv, self.side_send, self.side_recv, self.cut_send, self.cut_recv = sems[0:6]
        self.all_send = sems[6:8]
        self.p = lax.axis_index("pipe")
        self.me = lax.axis_index("dp")
        self.c = lax.rem(self.p, 2)
        self.x = lax.rem(self.me, 2)
        self.z = lax.div(self.me, 2)
        self.sibling = self.p + 1 - 2 * self.c
        self.across = lax.rem(self.p + 2, 4)
        self.partner = self.me + 1 - 2 * self.x

    def owner(self, work):
        if self.pairs == 4:
            work()
        else:
            pl.when(self.z < 4)(work)

    def half(self, core):
        return pl.ds(pl.multiple_of(128 * core, 128), 128)

    def quarter(self, side):
        return pl.ds(pl.multiple_of(128 * self.c + 64 * side, 64), 64)

    def core_copy(self, k):
        return mesh_copy(
            self.send.at[k, self.half(1 - self.c)],
            self.core.at[k],
            self.core_send.at[k],
            self.core_recv.at[k],
            self.sibling,
            self.me,
        )

    def side_copy(self, k):
        return mesh_copy(
            self.send.at[k, self.quarter(1 - self.x)],
            self.side.at[k],
            self.side_send.at[k],
            self.side_recv.at[k],
            self.p,
            self.partner,
        )

    def start_core(self, k):
        self.send[k] = self.acc[k].astype(BF16)
        self.core_copy(k).start()

    def start_side(self, k):
        self.core_copy(k).wait_recv()
        rows = self.half(self.c)
        self.send[k, rows] = (self.send[k, rows].astype(F32) + self.core[k].astype(F32)).astype(BF16)
        self.side_copy(k).start()

    def start_cut(self, k):
        self.side_copy(k).wait_recv()
        summed = self.send[k, self.quarter(self.x)].astype(F32) + self.side[k].astype(F32)
        self.cut[k] = summed.astype(BF16).reshape(self.cut.shape[1:])

        @self.owner
        def _():
            self.gather[k, self.z] = self.cut[k, self.z]

        def send_piece(j, carry):
            @pl.when(j != self.z)
            def _():
                mesh_copy(
                    self.cut.at[k, j],
                    self.gather.at[k, self.z],
                    self.cut_send.at[k],
                    self.cut_recv.at[k],
                    self.p,
                    2 * j + self.x,
                ).start()

            return carry

        lax.fori_loop(0, 4, send_piece, 0)

    def sum_pieces(self, k):
        @self.owner
        def _():
            await_bytes(self.gather.at[k, pl.ds(0, self.pairs - 1)], self.cut_recv.at[k])

            def add(j, total):
                return total + self.gather[k, j].astype(F32)

            zero = jnp.zeros(self.total.shape[1:], F32)
            self.total[k] = lax.fori_loop(0, self.pairs, add, zero).astype(BF16)

    def start_gather(self, k, place, recv, pipe, far=None):
        def send_piece(j, carry):
            local = (pipe == self.p) & (j == self.z)

            @pl.when(local)
            def _():
                pltpu.make_async_copy(self.total.at[k], place, recv).start()

            @pl.when(jnp.logical_not(local))
            def _():
                mesh_copy(self.total.at[k], place, self.all_send[0].at[k], recv, pipe, 2 * j + self.x).start()

            if far is not None:

                @pl.when(far)
                def _():
                    mesh_copy(
                        self.total.at[k], place, self.all_send[1].at[k], recv, self.across, 2 * j + self.x
                    ).start()

            return carry

        @self.owner
        def _():
            lax.fori_loop(0, self.pairs, send_piece, 0)

    def finish_sends(self, k, pipe, far=None):
        self.core_copy(k).wait_send()
        self.side_copy(k).wait_send()

        @self.owner
        def _():
            await_bytes(self.cut.at[k, pl.ds(0, 3)], self.cut_send.at[k])

            @pl.when(pipe == self.p)
            def _():
                await_bytes(self.gather.at[k, pl.ds(0, self.pairs - 1)], self.all_send[0].at[k])

            @pl.when(pipe != self.p)
            def _():
                await_bytes(self.gather.at[k], self.all_send[0].at[k])

            if far is not None:

                @pl.when(far)
                def _():
                    await_bytes(self.gather.at[k], self.all_send[1].at[k])

        if self.pairs > 4:

            @pl.when(self.z >= 4)
            def _():
                await_bytes(self.cut.at[k], self.cut_send.at[k])


class Direct:
    def __init__(self, dp, refs, sems):
        self.dp = dp
        self.acc, self.send, self.core, self.cut, self.gather, self.total = refs
        self.core_send, self.core_recv, self.cut_send, self.cut_recv, self.all_send = sems
        self.p = lax.axis_index("pipe")
        self.me = lax.axis_index("dp")
        self.c = lax.rem(self.p, 2)
        self.sibling = self.p + 1 - 2 * self.c
        self.goal = self.p - self.c

    def owner(self, work):
        if self.dp == 8:
            work()
        else:
            pl.when(self.me < 8)(work)

    def half(self, core):
        return pl.ds(pl.multiple_of(128 * core, 128), 128)

    def core_copy(self):
        source = self.send.at[self.half(1 - self.c)]
        return mesh_copy(source, self.core, self.core_send, self.core_recv, self.sibling, self.me)

    def start_core(self):
        self.send[...] = self.acc[...].astype(BF16)
        self.core_copy().start()

    def start_cut(self):
        self.core_copy().wait_recv()
        summed = self.send[self.half(self.c)].astype(F32) + self.core[...].astype(F32)
        self.cut[...] = summed.astype(BF16).reshape(self.cut.shape)

        @self.owner
        def _():
            self.gather[self.me] = self.cut[self.me]

        def send_piece(j, carry):
            @pl.when(j != self.me)
            def _():
                place = self.gather.at[self.me]
                mesh_copy(self.cut.at[j], place, self.cut_send, self.cut_recv, self.p, j).start()

            return carry

        lax.fori_loop(0, 8, send_piece, 0)

    def start_gather(self, land, recv):
        place = land.at[pl.ds(pl.multiple_of(128 * self.c + 16 * self.me, 16), 16)]

        def send_piece(j, carry):
            local = (self.c == 0) & (j == self.me)

            @pl.when(local)
            def _():
                pltpu.make_async_copy(self.total, place, recv).start()

            @pl.when(jnp.logical_not(local))
            def _():
                mesh_copy(self.total, place, self.all_send, recv, self.goal, j).start()

            return carry

        @self.owner
        def _():
            await_bytes(self.gather.at[pl.ds(0, self.dp - 1)], self.cut_recv)

            def add(j, total):
                return total + self.gather[j].astype(F32)

            self.total[...] = lax.fori_loop(0, self.dp, add, jnp.zeros(self.total.shape, F32)).astype(BF16)
            lax.fori_loop(0, self.dp, send_piece, 0)

    def finish_sends(self):
        self.core_copy().wait_send()

        @self.owner
        def _():
            await_bytes(self.cut.at[pl.ds(0, 7)], self.cut_send)

            @pl.when(self.c == 0)
            def _():
                await_bytes(self.gather.at[pl.ds(0, self.dp - 1)], self.all_send)

            @pl.when(self.c == 1)
            def _():
                await_bytes(self.gather, self.all_send)

        if self.dp > 8:

            @pl.when(self.me >= 8)
            def _():
                await_bytes(self.cut, self.cut_send)


def section_kernel(
    images,
    dp,
    mask_ref,
    turn_ref,
    dil_ref,
    tok_hbm,
    cot_hbm,
    win_hbm,
    gain_ref,
    shift_ref,
    bin_ref,
    bout_ref,
    table_ref,
    proj_hbm,
    down_hbm,
    window_hbm,
    lrow_hbm,
    lcol_hbm,
    perm_hbm,
    permt_hbm,
    pick_hbm,
    out_hbm,
    back_hbm,
    sum_in_hbm,
    sum_down_hbm,
    notes_hbm,
    land_in,
    land_down,
    notes_ref,
    proj_ref,
    down_ref,
    window_ref,
    lrow_ref,
    lcol_ref,
    perm_ref,
    permt_ref,
    pick_ref,
    nat_ref,
    xhat_ref,
    rstd_ref,
    qkv_ref,
    prob_ref,
    att_ref,
    act_ref,
    slope_ref,
    up_ref,
    inverse_ref,
    ones_ref,
    maskadd_ref,
    bias_ref,
    tab_ref,
    diag_ref,
    win_ref,
    small_ref,
    gs_ref,
    give_ref,
    load_ref,
    wide_acc,
    wide_send,
    wide_core,
    wide_side,
    wide_cut,
    wide_gather,
    wide_total,
    slim_acc,
    slim_send,
    slim_core,
    slim_side,
    slim_cut,
    slim_gather,
    slim_total,
    tall_send,
    tall_core,
    tall_cut,
    tall_gather,
    tall_total,
    note_send,
    note_core,
    note_side,
    note_all,
    note_far,
    load_sem,
    const_sems,
    win_sems,
    small_sems,
    give_send,
    give_recv,
    cross_send,
    cross_recv,
    wide_sems,
    slim_sems,
    tall_sems,
    land_sems,
    share_send,
    share_recv,
    side_send,
    side_recv,
    far_send,
    far_recv,
    note_sems,
):
    p = lax.axis_index("pipe")
    me = lax.axis_index("dp")
    core = lax.rem(p, 2)
    block = lax.div(p, 2)
    sibling = p + 1 - 2 * core
    across = lax.rem(p + 2, 4)
    first = core * images
    rows_own = images * PIX
    pair_rows = 2 * PIX
    wide = Pack(
        dp,
        (wide_acc.at[pl.ds(1, 1)], wide_send, wide_core, wide_side, wide_cut, wide_gather, wide_total),
        [wide_sems.at[n] for n in range(8)],
    )
    slim = Pack(
        dp,
        (slim_acc, slim_send, slim_core, slim_side, slim_cut, slim_gather, slim_total),
        [slim_sems.at[n] for n in range(8)],
    )
    tall = Direct(
        dp,
        (wide_acc.at[0], tall_send, tall_core, tall_cut, tall_gather, tall_total),
        [tall_sems.at[n] for n in range(5)],
    )

    constants = (
        (window_hbm, window_ref),
        (lrow_hbm, lrow_ref),
        (lcol_hbm, lcol_ref),
        (perm_hbm, perm_ref),
        (permt_hbm, permt_ref),
        (proj_hbm.at[block], proj_ref),
        (down_hbm.at[block], down_ref),
    )
    constants = [
        pltpu.make_async_copy(source, target, const_sems.at[n]) for n, (source, target) in enumerate(constants)
    ]
    pick_load = pltpu.make_async_copy(pick_hbm, pick_ref, const_sems.at[len(constants)])

    barrier = pltpu.get_barrier_semaphore()
    side = lax.rem(me, 2)
    pair_of = lax.div(me, 2)
    partner = me + 1 - 2 * side

    def greet_one(pipe, dp_index):
        pl.semaphore_signal(
            barrier, inc=1, device_id=(pipe, dp_index), device_id_type=pl.DeviceIdType.MESH
        )

    def greet(j, carry):
        greet_one(sibling, j)
        pl.when(j != me)(lambda: greet_one(p, j))
        pl.when(lax.rem(j, 2) == side)(lambda: greet_one(across, j))
        return carry

    lax.fori_loop(0, dp, greet, 0)

    mine = pl.ds(pl.multiple_of(core * rows_own, 16), rows_own)
    win_load = pltpu.make_async_copy(win_hbm.at[0], win_ref.at[core], load_sem.at[0])
    win_load.start()
    pick_load.start()
    tok_load = pltpu.make_async_copy(tok_hbm.at[mine], load_ref, load_sem.at[1])
    cot_load = pltpu.make_async_copy(cot_hbm.at[mine], load_ref, load_sem.at[1])
    pl.when(block == 0)(tok_load.start)
    pl.when(block == 1)(cot_load.start)
    for copy in constants:
        copy.start()
    small_ref[core, 0:1] = gain_ref[...].astype(F32)
    small_ref[core, 1:2] = shift_ref[...].astype(F32)
    small_ref[core, 2:3] = bout_ref[...].astype(F32)
    for part in range(3):
        small_ref[core, 3 + part : 4 + part] = bin_ref[:, part * 256 : part * 256 + 256].astype(F32)
    pl.semaphore_wait(barrier, 2 * dp - 1 + dp // 2)
    win_copy = mesh_copy(win_ref.at[core], win_ref.at[core], win_sems.at[0], win_sems.at[1], sibling, me)
    small_copy = mesh_copy(
        small_ref.at[core], small_ref.at[core], small_sems.at[0], small_sems.at[1], sibling, me
    )
    small_copy.start()
    win_load.wait()
    win_copy.start()

    tab_ref[...] = jnp.zeros_like(tab_ref)
    tab_ref[:, 0 : SPAN * SPAN] = table_ref[block].astype(F32)
    tab = tab_ref[...].astype(BF16)
    pick_load.wait()
    for turn in range(2):
        base = dot_nn(tab, pick_ref[turn]) * LOG2E
        for s in range(8):
            rows = pl.ds(turn * 8, 8)
            for half in range(2):
                ring = base[:, half * 256 : half * 256 + 256]
                ring = pltpu.roll(ring, s, 1) if s else ring
                diag_ref[2 * half, rows, s] = ring[:, 0:128]
                diag_ref[2 * half + 1, rows, s] = ring[:, 128:256]

    def spread(n, carry):
        lanes = lane_ids((8, 128))
        for half in range(2):
            for t in range(HALF // 8):
                shift = (8 * t) % 128
                x, z = diag_ref[2 * half, n], diag_ref[2 * half + 1, n]
                if 8 * t >= 128:
                    x, z = z, x
                if shift:
                    x, z = pltpu.roll(x, shift, 1), pltpu.roll(z, shift, 1)
                    x, z = jnp.where(lanes >= shift, x, z), jnp.where(lanes >= shift, z, x)
                rows = pl.ds(8 * t, 8)
                bias_ref[n, half, 0, rows] = x
                bias_ref[n, half, 1, rows] = z
        return carry

    lax.fori_loop(0, 16, spread, 0)
    tok_load.wait()

    def load_pair(pair):
        rows = load_ref[pl.ds(pair * pair_rows, pair_rows)].astype(F32)
        for n in range(2):
            one = rows[n * PIX : n * PIX + PIX]
            nat_ref[0, 2 * pair + n] = jnp.concatenate([one, jnp.zeros((8, 256), F32)], axis=0).astype(BF16)

    def late_start():
        head_of_row = lax.broadcasted_iota(jnp.int32, (128, 512), 0) // HEAD
        head_of_lane = lane_ids((128, 512)) // 128
        ones_ref[...] = jnp.where(head_of_row == head_of_lane, 1.0, 0.0).astype(BF16)
        diag_ref[...] = jnp.zeros_like(diag_ref)
        gs_ref[...] = jnp.zeros_like(gs_ref)
        wide_acc[...] = jnp.zeros_like(wide_acc)
        slim_acc[...] = jnp.zeros_like(slim_acc)
        for pair in range(1, images // 2):
            load_pair(pair)

    load_pair(0)
    pl.when(block == 1)(late_start)
    for copy in constants:
        copy.wait()
    await_bytes(small_ref.at[0], small_sems.at[1])
    await_bytes(win_ref.at[0], win_sems.at[1])

    def spacing(i):
        return jnp.maximum(dil_ref[block, first + i] - 1, 0)

    def mask_for(i):
        d = spacing(i)
        rows_valid = mask_ref[first + i, 0]
        for r in range(1, R_SIDE):
            rows_valid = rows_valid + mask_ref[first + i, r * C_SIDE]
        cols_valid = mask_ref[first + i, 0]
        for c in range(1, C_SIDE):
            cols_valid = cols_valid + mask_ref[first + i, c]
        for half in range(2):
            allowed = (lrow_ref[d, half] < rows_valid) & (lcol_ref[d, half] < cols_valid)
            shut = jnp.where(allowed, 0.0, NEG)[0:1]
            maskadd_ref[half] = window_ref[d, half].astype(F32) + shut

    def give_copies(kind, pair):
        target = pl.ds(pl.multiple_of(core * rows_own + pair * pair_rows, 16), pair_rows)
        target = (out_hbm, back_hbm)[kind // 2].at[0, target]
        source = give_ref.at[kind, pair, pl.ds(0, pair_rows)]
        recv = give_recv.at[kind // 2]
        remote = mesh_copy(source, target, give_send.at[kind, pair], recv, sibling, me)
        local = pltpu.make_async_copy(source, target, recv)
        return remote, local

    def cross_copy(i):
        return mesh_copy(nat_ref.at[0, i], nat_ref.at[1, i], cross_send.at[i], cross_recv.at[i], across, me)

    def record(kind, i, low):
        give_ref[kind, lax.div(i, 2), pl.ds(pl.multiple_of(lax.rem(i, 2) * PAD, 16), PAD)] = low

    def cross(kind, i):
        low = give_ref[kind, lax.div(i, 2), pl.ds(pl.multiple_of(lax.rem(i, 2) * PAD, 16), PAD)]
        nat_ref[0, i] = dot_nn(permt_ref[spacing(i)], low).astype(BF16) if kind == 1 else low
        cross_copy(i).start()

    def await_cross(i):
        await_bytes(nat_ref.at[1, i], cross_recv.at[i])

    def deliver(kind, pair):
        rows = []
        for n in range(2):
            low = give_ref[kind, pair, n * PAD : n * PAD + PAD]
            rows.append(dot_nn(permt_ref[spacing(2 * pair + n)], low)[0:PIX])
        give_ref[kind, pair, 0:pair_rows] = jnp.concatenate(rows, axis=0).astype(BF16)
        remote, local = give_copies(kind, pair)
        pl.when(core != kind % 2)(remote.start)
        pl.when(core == kind % 2)(local.start)

    def deliver_all(kind, start):
        def one(pair, carry):
            deliver(kind, pair)
            return carry

        lax.fori_loop(start, images // 2, one, 0)

    def forward(i):
        d = spacing(i)
        turn = turn_ref[first + i]
        mask_for(i)
        x = dot_nn(perm_ref[d], nat_ref[block, i])
        xhat, rstd = normalise(x)
        xhat_ref[0, i] = xhat
        rstd_ref[0, i] = rstd
        normed = (xhat * small_ref[0, 0:1] + small_ref[0, 1:2]).astype(BF16)
        mixed = dot_nn(normed, win_ref[0])
        scaled = (mixed[:, 0:256] + small_ref[0, 3:4]) * (HEAD**-0.5 * LOG2E)
        qkv_ref[i, :, 0:256] = scaled.astype(BF16)
        qkv_ref[i, :, 256:512] = (mixed[:, 256:512] + small_ref[0, 4:5]).astype(BF16)
        qkv_ref[i, :, 512:768] = (mixed[:, 512:768] + small_ref[0, 5:6]).astype(BF16)
        ones = jnp.ones((256, 128), BF16)
        attended = []
        inverse = []
        for half in range(2):
            yield True
            query = scaled[QUERY_AT[half] : QUERY_AT[half] + HALF].astype(BF16)
            key_rows = pl.ds(KEY_AT[half], 256)
            scores = dot_nt(mask_heads(query), qkv_ref[i, key_rows, 256:512])
            for h in range(HEADS):
                n = turn * 8 + h
                part = scores[h * HALF : (h + 1) * HALF]
                left = part[:, 0:128] + (bias_ref[n, half, 0] + maskadd_ref[half, :, 0:128])
                right = part[:, 128:256] + (bias_ref[n, half, 1] + maskadd_ref[half, :, 128:256])
                top = jnp.max(jnp.maximum(left, right), axis=-1, keepdims=True)
                rows = pl.ds(h * HALF, HALF)
                prob_ref[i, half, rows, 0:128] = jnp.exp2(left - top).astype(BF16)
                prob_ref[i, half, rows, 128:256] = jnp.exp2(right - top).astype(BF16)
            yield True
            values = []
            inverses = []
            for part in range(2):
                right = jnp.concatenate([qkv_ref[i, key_rows, 512 + part * 128 : 640 + part * 128], ones], axis=1)
                stack = dot_nn(prob_ref[i, half, pl.ds(part * 4 * HALF, 4 * HALF)], right)
                inverses.append(1.0 / pick_heads(stack[:, 128:256]))
                values.append(pick_heads(stack[:, 0:128]) * inverses[part])
            attended.append(jnp.concatenate(values, axis=1))
            inverse.append(jnp.where(lane_ids((HALF, 128)) % HEAD < 16, inverses[0], inverses[1]))
        att_ref[i] = join_halves(*attended).astype(BF16)
        inverse_ref[i] = join_halves(*inverse)
        yield True
        y = (x + dot_nn(att_ref[i], proj_ref[...]) + small_ref[0, 2:3]).astype(BF16)
        record(0, i, y)
        yield True
        x = y.astype(F32)
        xhat, rstd = normalise(x)
        xhat_ref[1, i] = xhat
        rstd_ref[1, i] = rstd
        normed = (xhat * small_ref[1, 0:1] + small_ref[1, 1:2]).astype(BF16)
        for part in range(3):
            yield True
            cols = slice(part * 256, part * 256 + 256)
            hidden = dot_nn(normed, win_ref[1, :, cols]) + small_ref[1, 3 + part : 4 + part]
            active, slope = gelu_pair(hidden)
            act_ref[i, :, cols] = active.astype(BF16)
            slope_ref[i, :, cols] = slope.astype(BF16)
        yield True
        z = (x + dot_nn(act_ref[i], down_ref[...]) + small_ref[1, 2:3]).astype(BF16)
        record(1, i, z)

    def norm_backward(i, t, g, dmix):
        dn = dot_nt(dmix, win_ref[t])
        xhat = xhat_ref[t, i]
        gs_ref[t, 0:1] += jnp.sum(dn * xhat, axis=0, keepdims=True)
        gs_ref[t, 1:2] += jnp.sum(dn, axis=0, keepdims=True)
        gs_ref[t, 2:3] += jnp.sum(g, axis=0, keepdims=True)
        e = dn * small_ref[t, 0:1]
        first_mean = jnp.mean(e, axis=-1, keepdims=True)
        second_mean = jnp.mean(e * xhat, axis=-1, keepdims=True)
        return (g + (e - first_mean - xhat * second_mean) * rstd_ref[t, i]).astype(BF16)

    def feed_backward(i, natural):
        g = dot_nn(perm_ref[spacing(i)], natural)
        low = g.astype(BF16)
        nat_ref[1, i] = low
        for part in range(3):
            yield True
            cols = slice(part * 256, part * 256 + 256)
            dact = dot_nt(low, down_ref[cols])
            dhidden = dact * slope_ref[i, :, cols].astype(F32)
            gs_ref[1, 3 + part : 4 + part] += jnp.sum(dhidden, axis=0, keepdims=True)
            slope_ref[i, :, cols] = dhidden.astype(BF16)
        yield True
        result = norm_backward(i, 1, g, slope_ref[i])
        up_ref[i] = result
        record(3, i, result)

    def attention_backward(i):
        turn = turn_ref[first + i].astype(F32)
        low = up_ref[i]
        packed = inverse_ref[i]
        lanes = lane_ids(packed.shape) % HEAD
        inverse = jnp.concatenate(
            [
                jnp.where(lanes < 16, packed, pltpu.roll(packed, 16, 1)),
                jnp.where(lanes < 16, pltpu.roll(packed, 112, 1), packed),
            ],
            axis=1,
        )
        datt_all = dot_nt(low, proj_ref[...]) * inverse
        attended = att_ref[i].astype(F32)
        query_all = qkv_ref[i, :, 0:256].astype(F32)
        dqueries = []
        dkvs = []
        for half in range(2):
            yield True
            rows_half = slice(QUERY_AT[half], QUERY_AT[half] + HALF)
            key_rows = pl.ds(KEY_AT[half], 256)
            datt32 = own_rows(datt_all[rows_half], half)
            datt = datt32.astype(BF16)
            query_t = query_all[rows_half].astype(BF16).T
            datt_t = datt.T
            dprob = dot_nt(mask_heads(datt), qkv_ref[i, key_rows, 512:768])
            products = (datt32 * attended[rows_half]).astype(BF16)
            totals = [dot_nn(products[:, part * 128 : part * 128 + 128], ones_ref[...]) for part in range(2)]
            dkeys = []
            dvalues = []
            ds = []
            for h in range(HEADS):
                rows = pl.ds(h * HALF, HALF)
                prob = prob_ref[i, half, rows]
                total = totals[h // 4][:, (h % 4) * 128 : (h % 4) * 128 + 128]
                part = dprob[h * HALF : (h + 1) * HALF]
                left = prob[:, 0:128].astype(F32) * (part[:, 0:128] - total)
                right = prob[:, 128:256].astype(F32) * (part[:, 128:256] - total)
                for kind, value in enumerate(diagonal_sums(left, right)):
                    diag_ref[2 * half + kind, h] += value * (1.0 - turn)
                    diag_ref[2 * half + kind, 8 + h] += value * turn
                ds.append(jnp.concatenate([left.astype(BF16), right.astype(BF16)], axis=1))
                head_rows = slice(h * HEAD, (h + 1) * HEAD)
                dkeys.append(dot_nn(query_t[head_rows], ds[h]))
                dvalues.append(dot_nn(datt_t[head_rows], prob))
            parts = []
            for part in range(2):
                keys = qkv_ref[i, key_rows, 256 + part * 128 : 384 + part * 128]
                parts.append(pick_heads(dot_nn(jnp.concatenate(ds[4 * part : 4 * part + 4], axis=0), keys)))
            dqueries.append(jnp.concatenate(parts, axis=1))
            yield True
            dkeys = jnp.concatenate(dkeys, axis=0).T * LN2
            dvalues = jnp.concatenate(dvalues, axis=0).T
            dkvs.append(jnp.concatenate([dkeys, dvalues], axis=1))
        yield True
        dquery = join_halves(*dqueries) * HEAD**-0.5
        dkv = jnp.concatenate([dkvs[0][0:32], dkvs[0][32:256] + dkvs[1][0:224], dkvs[1][224:256]], axis=0)
        gs_ref[0, 3:4] += jnp.sum(dquery, axis=0, keepdims=True)
        gs_ref[0, 4:5] += jnp.sum(dkv[:, 0:256], axis=0, keepdims=True)
        gs_ref[0, 5:6] += jnp.sum(dkv[:, 256:512], axis=0, keepdims=True)
        qkv_ref[i, :, 0:256] = dquery.astype(BF16)
        qkv_ref[i, :, 256:768] = dkv.astype(BF16)
        yield True
        result = norm_backward(i, 0, low.astype(F32), qkv_ref[i])
        record(2, i, result)

    def early_sides():
        slim.start_side(0)
        wide.start_side(0)

    def add_in(t, at, count):
        rows = count * PAD
        dmix = (qkv_ref, slope_ref)[t][pl.ds(at, count)].reshape(rows, 768)
        xhat = xhat_ref[t, pl.ds(at, count)].reshape(rows, 256)
        normed = (xhat * small_ref[t, 0:1] + small_ref[t, 1:2]).astype(BF16)
        wide_acc[t] += dot_tn(normed, dmix)

    def add_outer(at, count):
        rows = count * PAD
        up = nat_ref[1, pl.ds(at, count)].reshape(rows, 256)
        for part in range(3):
            cols = slice(part * 256, part * 256 + 256)
            slim_acc[0, :, cols] += dot_tn(act_ref[pl.ds(at, count), :, cols].reshape(rows, 256), up)
        after = up_ref[pl.ds(at, count)].reshape(rows, 256)
        slim_acc[0, :, 768:1024] += dot_tn(att_ref[pl.ds(at, count)].reshape(rows, 256), after)

    def add_feed(at, count):
        add_outer(at, count)
        add_in(1, at, count)

    def start_feed():
        slim.start_core(0)
        wide.start_core(0)

    def backward(i):
        yield from feed_backward(i, nat_ref[0, i])
        yield from attention_backward(i)

    def feed_and_sums(i):
        other = jnp.maximum(dil_ref[1, first + i] - 1, 0)
        yield from feed_backward(i, dot_nn(permt_ref[other], nat_ref[1, i]).astype(BF16))
        yield True
        add_feed(i, 1)

    def attention_and_sums(i):
        yield from attention_backward(i)
        yield True
        add_in(0, i, 1)

    def over(start, stop, work):
        def one(i, carry):
            work(i)
            return carry

        lax.fori_loop(start, stop, one, 0)

    def first_forward(i):
        pl.when(block == 1)(lambda: await_cross(i))
        together(forward(i))

        @pl.when(block == 0)
        def _():
            cross(1, i)
            pl.when(i == 0)(late_start)

            @pl.when(lax.rem(i, 2) == 1)
            def _():
                deliver(0, lax.div(i, 2))
                deliver(1, lax.div(i, 2))

    over(0, jnp.where(block == 0, images, 1), first_forward)

    def back_and_forth(i):
        await_cross(i + 1)
        together(backward(i), forward(i + 1))
        cross(2, i)

    over(0, jnp.where(block == 0, 0, images - 1), back_and_forth)

    def early_feed(i):
        await_cross(i)
        together(feed_and_sums(i))

        @pl.when(lax.rem(i, 2) == 1)
        def _():
            pl.when(i < images - 1)(lambda: deliver(3, lax.div(i, 2)))

    over(0, jnp.where(block == 0, LAG, 0), early_feed)

    def both_backward(i):
        await_cross(i)
        together(feed_and_sums(i), attention_and_sums(i - LAG))
        pl.when(lax.rem(i, 2) == 1)(lambda: deliver(3, lax.div(i, 2)))
        pl.when((lax.rem(i, 2) == 1) & (i >= 3))(lambda: deliver(2, lax.div(i - 3, 2)))

    over(LAG, jnp.where(block == 0, images - 1, LAG), both_backward)
    over(jnp.where(block == 0, images - 1, images), images, early_feed)

    @pl.when(block == 0)
    def _():
        start_feed()
        deliver(3, images // 2 - 1)
        deliver(2, images // 2 - 2)
        early_sides()
        together(attention_and_sums(images - 2), attention_and_sums(images - 1))
        slim.start_cut(0)

    @pl.when(block == 1)
    def _():
        together(backward(images - 1))
        cross(2, images - 1)
        over(0, images // 4, lambda n: add_outer(4 * n, 4))
        slim.start_core(0)
        over(0, images // 4, lambda n: add_in(1, 4 * n, 4))
        wide.start_core(0)
        slim.start_side(0)
        over(0, images // 4, lambda n: add_in(0, 4 * n, 4))
        tall.start_core()
        wide.start_side(0)
        deliver_all(3, 0)
        slim.start_cut(0)
        deliver_all(0, 0)

    piece_rows = pl.ds(pl.multiple_of(pair_of * 16, 16), 16)
    quarter_rows = pl.ds(pl.multiple_of(128 * core + 64 * side + 16 * pair_of, 16), 16)
    far = block == 0
    pl.when(block == 0)(tall.start_core)
    wide.start_cut(0)

    table_sum = jnp.zeros((8, 256), F32)
    for turn in range(2):
        rows = pl.ds(turn * 8, 8)
        sums = []
        for half in range(2):
            total = jnp.zeros((8, 256), F32)
            for s in range(8):
                ring = jnp.concatenate([diag_ref[2 * half, rows, s], diag_ref[2 * half + 1, rows, s]], axis=1)
                total = total + (pltpu.roll(ring, 256 - s, 1) if s else ring)
            sums.append(total)
        sums = jnp.concatenate(sums, axis=1)
        upper = sums.astype(BF16)
        lower = (sums - upper.astype(F32)).astype(BF16)
        table_sum = table_sum + dot_nt(upper, pick_ref[turn]) + dot_nt(lower, pick_ref[turn])

    note_send[0:8] = gs_ref[1 - core]
    note_send[8:16] = table_sum
    note_core[core, 0:8] = gs_ref[core]
    note_core[core, 8:16] = table_sum
    note_copy = mesh_copy(note_send, note_core.at[core], note_sems.at[0], note_sems.at[1], sibling, me)
    note_copy.start()
    tall.start_cut()
    slim.sum_pieces(0)
    slim.start_gather(0, land_down.at[block, core, side, piece_rows], land_sems.at[1, block], p, far)
    wide.sum_pieces(0)
    wide.start_gather(0, land_in.at[quarter_rows], land_sems.at[0, 1], 2 * block + 1)
    note_copy.wait_recv()
    note_side[side] = note_core[0] + note_core[1]
    side_copy = mesh_copy(note_side.at[side], note_side.at[side], note_sems.at[2], note_sems.at[3], p, partner)
    side_copy.start()

    def side_share(b):
        land = land_down.at[b, core, side]
        return mesh_copy(land, land, side_send.at[0, b], side_recv.at[0, b], p, partner)

    def side_start(b):
        await_bytes(land_down.at[b, 0, 0], land_sems.at[1, b])
        side_share(b).start()

    side_start(block)
    deliver_all(2, jnp.where(block == 0, LATE_PAIR, 0))
    deliver_all(1, jnp.where(block == 0, images // 2, 0))
    side_copy.wait_recv()
    note_all[pair_of] = note_side[0] + note_side[1]

    def send_note(j, carry):
        @pl.when(j != pair_of)
        def _():
            place = note_all.at[pair_of]
            mesh_copy(place, place, note_sems.at[4], note_sems.at[5], p, 2 * j + side).start()

        return carry

    lax.fori_loop(0, dp // 2, send_note, 0)

    def share_copy(b):
        land = land_down.at[b, core]
        return mesh_copy(land, land, share_send.at[b], share_recv.at[b], sibling, me)

    tall.start_gather(land_in, land_sems.at[0, 0])
    def cross_share():
        land = land_down.at[1, core]
        return mesh_copy(land, land, far_send, far_recv, across, me)

    def in_copies():
        copies = []
        for c in range(2):
            rows = land_in.at[pl.ds(pl.multiple_of(128 * c + 64 * side, 64), 64)]
            copies.append(mesh_copy(rows, rows, side_send.at[2, c], side_recv.at[2, c], p, partner))
        return copies

    @pl.when(core == 1)
    def _():
        await_bytes(land_in.at[0:128], land_sems.at[0, 1])
        for copy in in_copies():
            copy.start()

    side_share(block).wait_recv()
    share_copy(block).start()
    pl.when(block == 1)(lambda: cross_share().start())
    await_bytes(note_all.at[pl.ds(0, dp // 2 - 1)], note_sems.at[5])

    def add_note(j, total):
        return total + note_all[j]

    notes = lax.fori_loop(0, dp // 2, add_note, jnp.zeros((16, 256), F32))
    notes_ref[0] = notes[0:8]
    note_far[0] = notes[8:16]
    far_copy = mesh_copy(note_far.at[0], note_far.at[1], note_sems.at[6], note_sems.at[7], across, me)
    far_copy.start()

    @pl.when(block == 1)
    def _():
        side_start(0)
        side_share(0).wait_recv()

    pl.when(block == 0)(lambda: cross_share().wait_recv())
    share_copy(1 - block).start()
    far_copy.wait_recv()
    notes_ref[1 + block] = note_far[0]
    notes_ref[2 - block] = note_far[1]
    notes_copy = pltpu.make_async_copy(notes_ref, notes_hbm, load_sem.at[4])
    notes_copy.start()

    pl.when(core == 0)(lambda: await_bytes(land_in, land_sems.at[0, 0]))

    @pl.when(core == 1)
    def _():
        for copy in in_copies():
            copy.wait()

    results = [notes_copy, pltpu.make_async_copy(land_in, sum_in_hbm, load_sem.at[0])]
    results[1].start()
    for b in (1, 0):
        share_copy(b).wait()
        results.append(pltpu.make_async_copy(land_down.at[b], sum_down_hbm.at[b], load_sem.at[2 + b]))
        results[-1].start()
    await_bytes(out_hbm, give_recv.at[0])
    await_bytes(back_hbm, give_recv.at[1])
    for kind in range(4):

        @pl.when(core != kind % 2)
        def _(kind=kind):
            for pair in range(images // 2):
                give_copies(kind, pair)[0].wait_send()

    for i in range(images):
        cross_copy(i).wait_send()
    win_copy.wait_send()
    small_copy.wait_send()
    note_copy.wait_send()
    side_copy.wait_send()
    far_copy.wait_send()
    await_bytes(note_all.at[pl.ds(0, dp // 2 - 1)], note_sems.at[4])
    side_share(block).wait_send()

    @pl.when(block == 1)
    def _():
        side_share(0).wait_send()
        cross_share().wait_send()

    for copy in results:
        copy.wait()
    tall.finish_sends()
    wide.finish_sends(0, 2 * block + 1)
    slim.finish_sends(0, p, far)


def result_kernel(
    out_raw,
    back_raw,
    sum_in,
    sum_down,
    notes_hbm,
    out_hbm,
    back_hbm,
    g_in_hbm,
    g_proj_hbm,
    g_down_hbm,
    g_gain_hbm,
    g_shift_hbm,
    g_bin_hbm,
    g_bout_hbm,
    g_table_hbm,
    out_buf,
    back_buf,
    in_buf,
    down_buf,
    notes,
    g_in,
    g_proj,
    g_down,
    g_gain,
    g_shift,
    g_bin,
    g_bout,
    g_table,
    load_sems,
    store_sems,
    part_sems,
):
    low = [(notes_hbm, notes), (sum_in, in_buf), (sum_down, down_buf)]
    sums = [pltpu.make_async_copy(source, target, load_sems.at[n]) for n, (source, target) in enumerate(low)]
    rows = out_buf.shape[0] // 4
    loads = []
    stores = []
    for part in range(4):
        at = pl.ds(part * rows, rows)
        for n, (raw, buf, target) in enumerate(((out_raw, out_buf, out_hbm), (back_raw, back_buf, back_hbm))):
            loads.append(pltpu.make_async_copy(raw.at[0, at], buf.at[at], part_sems.at[0, n, part]))
            stores.append(pltpu.make_async_copy(buf.at[at], target.at[0, at], part_sems.at[1, n, part]))
    for copy in sums + loads:
        copy.start()
    full = [
        (g_gain, g_gain_hbm),
        (g_shift, g_shift_hbm),
        (g_bin, g_bin_hbm),
        (g_bout, g_bout_hbm),
        (g_table, g_table_hbm),
        (g_in, g_in_hbm.at[0]),
        (g_proj, g_proj_hbm),
        (g_down, g_down_hbm),
    ]
    finals = [pltpu.make_async_copy(source, target, store_sems.at[n]) for n, (source, target) in enumerate(full)]
    sums[0].wait()
    g_gain[...] = notes[0, 0:1]
    g_shift[...] = notes[0, 1:2]
    g_bout[...] = notes[0, 2:3]
    for part in range(3):
        cols = slice(part * 256, part * 256 + 256)
        g_bin[:, cols] = notes[0, 3 + part : 4 + part]
    for b in range(2):
        g_table[b] = notes[1 + b, :, 0 : SPAN * SPAN]
    for copy in finals[0:5]:
        copy.start()
    sums[1].wait()
    g_in[...] = in_buf[...].astype(F32)
    finals[5].start()
    sums[2].wait()
    for b in range(2):
        g_proj[b] = down_buf[b, :, :, :, 768:1024].reshape(256, 256).astype(F32)
        for part in range(3):
            cols = slice(part * 256, part * 256 + 256)
            g_down[b, cols] = down_buf[b, :, :, :, cols].reshape(256, 256).astype(F32)
    finals[6].start()
    finals[7].start()
    for load, store in zip(loads, stores):
        load.wait()
        store.start()
    for store in finals + stores:
        store.wait()


def run_kernels(dp, images, smem_operands, hbm_operands, vmem_operands):
    tables = [jnp.asarray(t) for t in constant_tables()]
    rows = images * PIX
    vmem = pl.BlockSpec(memory_space=pltpu.VMEM)
    smem = pl.BlockSpec(memory_space=pltpu.SMEM)
    hbm = pl.BlockSpec(memory_space=pl.ANY)
    dma = pltpu.SemaphoreType.DMA
    raw_shape = (
        jax.ShapeDtypeStruct((1, 2 * rows, 256), BF16),
        jax.ShapeDtypeStruct((1, 2 * rows, 256), BF16),
        jax.ShapeDtypeStruct((256, 768), BF16),
        jax.ShapeDtypeStruct((2, 2, 2, 64, 1024), BF16),
        jax.ShapeDtypeStruct((3, 8, 256), F32),
    )
    out_shape = raw_shape[0:2] + (
        jax.ShapeDtypeStruct((1, 256, 768), F32),
        jax.ShapeDtypeStruct((2, 256, 256), F32),
        jax.ShapeDtypeStruct((2, 768, 256), F32),
        jax.ShapeDtypeStruct((1, 256), F32),
        jax.ShapeDtypeStruct((1, 256), F32),
        jax.ShapeDtypeStruct((1, 768), F32),
        jax.ShapeDtypeStruct((1, 256), F32),
        jax.ShapeDtypeStruct((2, HEADS, SPAN * SPAN), F32),
    )

    def pack(sums, count, columns):
        return [
            pltpu.VMEM((sums, 256, columns), F32),
            pltpu.VMEM((count, 256, columns), BF16),
            pltpu.VMEM((count, 128, columns), BF16),
            pltpu.VMEM((count, 64, columns), BF16),
            pltpu.VMEM((count, 4, 16, columns), BF16),
            pltpu.VMEM((count, dp // 2, 16, columns), BF16),
            pltpu.VMEM((count, 16, columns), BF16),
        ]

    scratch = [
        *[pltpu.VMEM(shape.shape, shape.dtype) for shape in raw_shape[2:5]],
        pltpu.VMEM((256, 256), BF16),
        pltpu.VMEM((768, 256), BF16),
        *[pltpu.VMEM(table.shape, table.dtype) for table in tables],
        pltpu.VMEM((2, images, PAD, 256), BF16),
        pltpu.VMEM((2, images, PAD, 256), F32),
        pltpu.VMEM((2, images, PAD, 1), F32),
        pltpu.VMEM((images, PAD, 768), BF16),
        pltpu.VMEM((images, 2, HEADS * HALF, 256), BF16),
        pltpu.VMEM((images, PAD, 256), BF16),
        pltpu.VMEM((images, PAD, 768), BF16),
        pltpu.VMEM((images, PAD, 768), BF16),
        pltpu.VMEM((images, PAD, 256), BF16),
        pltpu.VMEM((images, PAD, 128), F32),
        pltpu.VMEM((128, 512), BF16),
        pltpu.VMEM((2, HALF, 256), F32),
        pltpu.VMEM((16, 2, 2, HALF, 128), F32),
        pltpu.VMEM((8, 256), F32),
        pltpu.VMEM((4, 16, 8, 128), F32),
        pltpu.VMEM((2, 256, 768), BF16),
        pltpu.VMEM((2, 8, 256), F32),
        pltpu.VMEM((2, 8, 256), F32),
        pltpu.VMEM((4, images // 2, 2 * PAD, 256), BF16),
        pltpu.VMEM((rows, 256), BF16),
        *pack(2, 1, 768),
        *pack(1, 1, 1024),
        pltpu.VMEM((256, 768), BF16),
        pltpu.VMEM((128, 768), BF16),
        pltpu.VMEM((8, 16, 768), BF16),
        pltpu.VMEM((dp, 16, 768), BF16),
        pltpu.VMEM((16, 768), BF16),
        pltpu.VMEM((16, 256), F32),
        pltpu.VMEM((2, 16, 256), F32),
        pltpu.VMEM((2, 16, 256), F32),
        pltpu.VMEM((dp // 2, 16, 256), F32),
        pltpu.VMEM((2, 8, 256), F32),
        dma((6,)),
        dma((8,)),
        dma((2,)),
        dma((2,)),
        dma((4, images // 2)),
        dma((2,)),
        dma((images,)),
        dma((images,)),
        dma((8, 1)),
        dma((8, 1)),
        dma((5,)),
        dma((3, 2)),
        dma((2,)),
        dma((2,)),
        dma((3, 2)),
        dma((3, 2)),
        dma,
        dma,
        dma((8,)),
    ]
    raw = pl.pallas_call(
        functools.partial(section_kernel, images, dp),
        out_shape=raw_shape,
        in_specs=[smem] * 3 + [hbm] * 3 + [vmem] * 5 + [hbm] * 8,
        out_specs=[hbm] * 5,
        scratch_shapes=scratch,
        compiler_params=pltpu.CompilerParams(
            vmem_limit_bytes=63 * 1024 * 1024, collective_id=0, has_side_effects=True
        ),
    )(*smem_operands, *hbm_operands, *vmem_operands, *tables)
    return pl.pallas_call(
        result_kernel,
        out_shape=out_shape,
        in_specs=[hbm] * 5,
        out_specs=[hbm] * 10,
        scratch_shapes=[
            pltpu.VMEM((2 * rows, 256), BF16),
            pltpu.VMEM((2 * rows, 256), BF16),
            *[pltpu.VMEM(shape.shape, shape.dtype) for shape in raw_shape[2:5]],
            pltpu.VMEM((256, 768), F32),
            *[pltpu.VMEM(shape.shape, F32) for shape in out_shape[3:10]],
            dma((3,)),
            dma((8,)),
            dma((2, 2, 4)),
        ],
        compiler_params=pltpu.CompilerParams(vmem_limit_bytes=63 * 1024 * 1024),
    )(*raw)


def body(
    tokens_in,
    cotangent,
    valid_mask,
    orientation,
    dilation,
    norm_gain,
    norm_bias,
    in_weight,
    in_bias,
    out_bias,
    proj_weight,
    down_weight,
    position_bias,
):
    images = valid_mask.shape[0] // 2
    results = run_kernels(
        lax.axis_size("dp"),
        images,
        (valid_mask, orientation, dilation.T),
        (tokens_in, cotangent, in_weight),
        (norm_gain, norm_bias, in_bias, out_bias, position_bias, proj_weight, down_weight),
    )
    out, back, g_in, g_proj, g_down, g_gain, g_shift, g_bin, g_bout, g_table = results
    return out, back, g_gain, g_shift, g_in, g_bin, g_bout, g_proj, g_down, g_table


def solution(mesh):
    placed = (
        P("dp", None),
        P("dp", None),
        P("dp", None),
        P("dp"),
        P("dp", None),
        P("pipe", None),
        P("pipe", None),
        P("pipe", None, None),
        P("pipe", None),
        P("pipe", None),
        P(),
        P(),
        P(),
    )
    return jax.shard_map(
        body,
        mesh=mesh,
        in_specs=placed,
        out_specs=(
            P("pipe", "dp", None),
            P("pipe", "dp", None),
            P("pipe", None),
            P("pipe", None),
            P("pipe", None, None),
            P("pipe", None),
            P("pipe", None),
            P(),
            P(),
            P(),
        ),
        check_vma=False,
    )
```
